128 devices in a mesh: row: 16 (over y, x), col: 8 (over z, core).
Axes of the slice: x: 4, y: 4, z: 4, core: 2. Of those that a mesh axis runs over, the one named last changes fastest.
Arguments:
- embeddings: bfloat16 [24576, 1024], P(None, ('row', 'col')), may hold values from -6 to 6
- inv_scale: float32 [1024], replicated, may hold values from 0.5 to 2
- noise: float32 [24576], replicated, may hold values from 0.5 to 2
Outputs:
- factor: float32 [12, 16, 128, 1024], P(None, 'row', None, 'col')
- schur: float32 [12, 16, 128, 24, 8, 128], P(None, 'row', None, None, 'col')
The draws below stay inside these ranges and needn't reach their ends.
All inputs are finite; a program needn't handle non-finite values.
Results may differ from the reference program's by a relative error of at most 0.0027.
Values may be sent and summed in bfloat16 or wider, within the bound.
A program may use at most 192 MiB of HBM per device.

```python
import math
import jax
import jax.numpy as jnp
from jax import lax

N = 24576
F = 1024
TILE = 128
PB = 512
PANELS = 2
GRID_ROWS = 16
GRID_COLS = 8
ROW_CYC = 12
COL_CYC = 24


def levels(own_key, shape, split, low, largest):
    loudness, own = 1.0, jax.random.fold_in(own_key, 6)
    for axis_at, parts in split:
        steps = jnp.exp(jax.random.uniform(jax.random.fold_in(own, axis_at), (parts,), jnp.float32, low / len(split), largest / len(split)))
        loudness = loudness * jnp.repeat(steps, shape[axis_at] // parts).reshape([-1 if axis == axis_at else 1 for axis in range(len(shape))])
    return loudness


def normal_values(rng, shape, width, limit, cuts=(), dtype=jnp.bfloat16):
    factor_of = levels(rng, shape, cuts, -0.22, 0.18) if cuts else 1.0
    values = jax.random.normal(rng, shape, jnp.float32) * width * factor_of
    return jnp.minimum(jnp.maximum(values, -limit), limit).astype(dtype)


def setup_inputs(seed: int = 0) -> dict:
    arg_keys = jax.random.split(jax.random.key(seed), 4)
    return {
        "embeddings": normal_values(arg_keys[0], (N, F), 1.0, 6.0, ((1, 128),)),
        "inv_scale": jnp.clip(jnp.exp(jax.random.uniform(arg_keys[1], (F,), jnp.float32, math.log(0.5), math.log(2.0))), 0.5, 2.0),
        "noise": jnp.clip(jnp.exp(jax.random.uniform(arg_keys[2], (N,), jnp.float32, math.log(0.5), math.log(2.0))), 0.5, 2.0),
    }


def kernel_rows(rows_z, rows_sq, rows_idx, rows_noise, cols_z, cols_sq, cols_idx):
    inner = jnp.dot(rows_z.astype(jnp.float32), cols_z.T.astype(jnp.float32), preferred_element_type=jnp.float32)
    dist = rows_sq[:, None] + cols_sq[None, :] - 2.0 * inner
    kern = jnp.exp(dist * (-0.5 / F))
    same = rows_idx[:, None] == cols_idx[None, :]
    return kern + jnp.where(same, rows_noise[:, None], jnp.zeros_like(kern))

def reference(embeddings, inv_scale, noise):
    scaled = (embeddings.astype(jnp.float32) * inv_scale).astype(jnp.bfloat16)
    sq = jnp.sum(jnp.square(scaled.astype(jnp.float32)), axis=1)
    index = jnp.arange(N).astype(jnp.int32)
    lead = PANELS * PB
    leading = kernel_rows(scaled, sq, index, noise, scaled[:lead], sq[:lead], index[:lead])
    factors = []
    for k in range(PANELS):
        column = leading[:, k * PB:(k + 1) * PB]
        for prev in factors:
            column = column - jnp.dot(prev, prev[k * PB:(k + 1) * PB].T, precision=lax.Precision.HIGHEST)
        column = jnp.where((index < k * PB)[:, None], jnp.zeros_like(column), column)
        chol = jnp.linalg.cholesky(column[k * PB:(k + 1) * PB])
        factors.append(jax.scipy.linalg.solve_triangular(chol, column.T, lower=True).T)
    factor = jnp.concatenate(factors, axis=1)
    block = N // GRID_ROWS

    def one_block(number):
        start = (number * block).astype(jnp.int32)
        rows_z = lax.dynamic_slice_in_dim(scaled, start, block, 0)
        rows_sq = lax.dynamic_slice_in_dim(sq, start, block, 0)
        rows_idx = lax.dynamic_slice_in_dim(index, start, block, 0)
        rows_noise = lax.dynamic_slice_in_dim(noise, start, block, 0)
        rows_l = lax.dynamic_slice_in_dim(factor, start, block, 0)
        kern = kernel_rows(rows_z, rows_sq, rows_idx, rows_noise, scaled, sq, index)
        return kern - jnp.dot(rows_l, factor.T, precision=lax.Precision.HIGHEST)
    schur = lax.map(one_block, jnp.arange(GRID_ROWS).astype(jnp.int32)).reshape(N, N)
    dead = (index[:, None] < lead) | (index[None, :] < lead)
    schur = jnp.where(dead, jnp.zeros_like(schur), schur)
    factor_out = factor.reshape(ROW_CYC, GRID_ROWS, TILE, lead)
    schur_out = schur.reshape(ROW_CYC, GRID_ROWS, TILE, COL_CYC, GRID_COLS, TILE)
    return (factor_out, schur_out)
```

```python
import functools
import math

import jax
import jax.numpy as jnp
from jax import lax
from jax.experimental import pallas as pl
from jax.experimental.pallas import tpu as pltpu
from jax.sharding import PartitionSpec as P

TILE = 128
PB = 512
PANELS = 2
B=128
def factor_block(load, store):
    lane = lax.broadcasted_iota(jnp.int32, (8, B), 1)
    sub = lax.broadcasted_iota(jnp.int32, (8, B), 0)
    X = [load(g) for g in range(B // 8)]
    for g in range(B // 8):
        P = X[g]
        base = 8 * g
        c = [jnp.broadcast_to(P[:, base + j:base + j + 1], (8, B)) for j in range(8)]
        s = [[jnp.broadcast_to(c[j][i:i + 1, :], (8, B)) if j <= i else None for j in range(8)] for i in range(8)]
        ingroup = (lane >= base) & (lane < base + 8)
        Pp = jnp.where(ingroup, jnp.where(lane - base == sub, 1.0, 0.0), P)
        r = [jnp.broadcast_to(Pp[k:k + 1, :], (8, B)) for k in range(8)]
        l = [[None] * 8 for _ in range(8)]
        dinv = [None] * 8
        for k in range(8):
            dinv[k] = 1.0 / s[k][k]
            for i in range(k + 1, 8):
                l[i][k] = s[i][k] * dinv[k]
                for j in range(k + 1, i + 1):
                    s[i][j] = s[i][j] - l[i][k] * s[j][k]
        f = []
        for k in range(8):
            v = r[k]
            for m in range(k):
                v = v - l[k][m] * f[m]
            f.append(v)
        w = [None] * 8
        for k in range(7, -1, -1):
            v = f[k] * dinv[k]
            for m in range(k + 1, 8):
                v = v - l[m][k] * w[m]
            w[k] = v
        fo, so = f[0], s[0][0]
        for k in range(1, 8):
            fo = jnp.where(sub == k, f[k], fo)
            so = jnp.where(sub == k, s[k][k], so)
        store(g, fo * lax.rsqrt(so))
        for i in range(g + 1, B // 8):
            Xi = X[i]
            acc = jnp.where(ingroup, 0.0, Xi)
            for k in range(8):
                acc = acc - jnp.broadcast_to(Xi[:, base + k:base + k + 1], (8, B)) * w[k]
            X[i] = acc

def split(x):
    hi = x.astype(jnp.bfloat16)
    return hi, (x - hi.astype(jnp.float32)).astype(jnp.bfloat16)

def dot(a, b):
    return jnp.dot(a, b, preferred_element_type=jnp.float32)

def dot3(a, b):
    ah, al = a; bh, bl = b
    return dot(ah, bh) + dot(ah, bl) + dot(al, bh)

LOG2E = math.log2(math.e)

def chol_body(zl_ref, noise_ref, w_ref, wt_ref, X, V, zt, n, width):
    nb = n // B
    zt[...] = zl_ref[...].T
    zf = zl_ref[...].astype(jnp.float32)
    hc = jnp.sum(zf * zf, axis=0, keepdims=True) * (LOG2E / (2 * width))
    hcol = jnp.broadcast_to(hc, (8, n)).T[:, 0:1]
    for i in range(nb):
        rows = slice(i * B, (i + 1) * B)
        t = dot(zt[rows, :], zl_ref[...]) * (LOG2E / width) - hcol[rows, :] - hc
        k = jnp.exp2(t)
        ri = lax.broadcasted_iota(jnp.int32, (B, n), 0) + i * B
        ci = lax.broadcasted_iota(jnp.int32, (B, n), 1)
        X[rows, :] = k + jnp.where(ri == ci, jnp.broadcast_to(noise_ref[...], (B, n)), 0.0)
    tri = lax.broadcasted_iota(jnp.int32, (B, B), 0) >= lax.broadcasted_iota(jnp.int32, (B, B), 1)
    eye = jnp.where(lax.broadcasted_iota(jnp.int32, (B, B), 0) == lax.broadcasted_iota(jnp.int32, (B, B), 1), 1.0, 0.0)

    def step(b, _):
        r0 = pl.multiple_of(b * B, B)
        def load(g):
            return X[pl.ds(r0 + 8 * g, 8), pl.ds(r0, B)]
        def store(g, v):
            V[pl.ds(8 * g, 8), :] = v
        factor_block(load, store)
        v = jnp.where(tri, V[...], 0.0)
        X[pl.ds(r0, B), pl.ds(r0, B)] = eye
        P = dot3(split(v), split(X[pl.ds(r0, B), :]))
        X[pl.ds(r0, B), :] = P
        Ps = split(P)
        def upd(i, _):
            i0 = pl.multiple_of(i * B, B)
            T = X[pl.ds(r0, B), pl.ds(i0, B)].T
            X[pl.ds(i0, B), pl.ds(r0, B)] = jnp.zeros((B, B), jnp.float32)
            X[pl.ds(i0, B), :] = X[pl.ds(i0, B), :] - dot3(split(T), Ps)
            return 0
        lax.fori_loop(b + 1, nb, upd, 0)
        return 0
    lax.fori_loop(0, nb, step, 0)
    for i in range(nb):
        rows = slice(i * B, (i + 1) * B)
        ri = lax.broadcasted_iota(jnp.int32, (B, n), 0) + i * B
        ci = lax.broadcasted_iota(jnp.int32, (B, n), 1)
        w = jnp.where(ri >= ci, X[rows, :], 0.0)
        h, lo = split(w)
        w_ref[0, rows, :] = h; w_ref[1, rows, :] = lo
        wt_ref[0, :, rows] = h.T; wt_ref[1, :, rows] = lo.T

def chol_call(zl, noise):
    width, n = zl.shape
    def k(zl_ref, noise_ref, w_ref, wt_ref, X, V, zt):
        chol_body(zl_ref, noise_ref, w_ref, wt_ref, X, V, zt, n, width)
    o = jax.ShapeDtypeStruct((2, n, n), jnp.bfloat16)
    return pl.pallas_call(k, out_shape=(o, o),
        in_specs=[pl.BlockSpec(memory_space=pltpu.VMEM)]*2,
        out_specs=[pl.BlockSpec(memory_space=pltpu.VMEM)]*2,
        scratch_shapes=[pltpu.VMEM((n, n), jnp.float32), pltpu.VMEM((B, B), jnp.float32), pltpu.VMEM((n, width), jnp.bfloat16)],
        compiler_params=pltpu.CompilerParams(vmem_limit_bytes=60*2**20))(zl, noise)

B=128
bf16=jnp.bfloat16; f32=jnp.float32

def main_body(pos_ref, zl_ref, zr_ref, zc_ref, w_ref, wt_ref, nz_ref, out_ref, fac_ref,
              zlt, zrt, kh, kl, lh, ll, gh, gl, g1, hr, hlc, stage, sem, *, width, lead, nrow, ncol, passes, RT=512, CT=256):
    rows = zr_ref.shape[1]; cols = zc_ref.shape[1]
    p = pos_ref[0]; q = pos_ref[1]
    cs = LOG2E / (2 * width)
    for i in range(0, lead, 256):
        zlt[i:i+256, :] = zl_ref[:, i:i+256].T
    def colsq(ref, sl):
        x = ref[:, sl].astype(f32)
        return jnp.sum(x * x, axis=0, keepdims=True) * cs
    def lanecol(v):
        return jnp.broadcast_to(jnp.broadcast_to(v, (8, v.shape[1])).T[:, 0:1], (v.shape[1], B))
    for i in range(0, rows, 256):
        zrt[i:i+256, :] = zr_ref[:, i:i+256].T
        hr[i:i+256, :] = lanecol(colsq(zr_ref, slice(i, i+256)))
    for i in range(0, lead, 256):
        hlc[i:i+256, :] = lanecol(colsq(zl_ref, slice(i, i+256)))
    def wide(x, n):
        return jnp.concatenate([x] * (n // B), axis=1)
    for j in range(0, lead, 256):
        hl = colsq(zl_ref, slice(j, j + 256))
        for i in range(0, rows, RT):
            t = dot(zrt[i:i+RT, :], zl_ref[:, j:j+256]) * (2 * cs) - wide(hr[i:i+RT, :], 256) - hl
            k = jnp.exp2(t)
            if i == 0:
                ri = lax.broadcasted_iota(jnp.int32, (B, 256), 0) + p * B
                ci = lax.broadcasted_iota(jnp.int32, (B, 256), 1) + j
                nug = jnp.where(ri == ci, jnp.broadcast_to(nz_ref[:, j:j+256], (B, 256)), 0.0)
                k = jnp.concatenate([k[:B] + nug, k[B:]], axis=0)
            h, l = split(k)
            kh[i:i+RT, j:j+256] = h
            kl[i:i+RT, j:j+256] = l
    for j in range(0, lead, 256):
        e = j + 256
        for i in range(0, rows, RT):
            rs = slice(i, i + RT)
            x = dot(kh[rs, :e], wt_ref[0, :e, j:e]) + dot(kh[rs, :e], wt_ref[1, :e, j:e]) + dot(kl[rs, :e], wt_ref[0, :e, j:e])
            h, l = split(x)
            lh[rs, j:e] = h
            ll[rs, j:e] = l
            for half in range(2):
                @pl.when(q == j // B + half)
                def _():
                    y = x[:, half * B:(half + 1) * B]
                    if i == 0:
                        ri = lax.broadcasted_iota(jnp.int32, (B, B), 0) + p * B
                        ci = lax.broadcasted_iota(jnp.int32, (B, B), 1) + (j + half * B)
                        y = jnp.concatenate([jnp.where(ri >= ci, y[:B], 0.0), y[B:]], axis=0)
                    fac_ref[rs, :] = y
    for i in range(0, rows, RT):
        rs = slice(i, i + RT)
        tot = None
        for j in range(0, lead, 256):
            x = dot(lh[rs, j:], w_ref[0, j:, j:j+256]) + dot(lh[rs, j:], w_ref[1, j:, j:j+256]) + dot(ll[rs, j:], w_ref[0, j:, j:j+256])
            h, l = split(x)
            gh[rs, j:j+256] = h
            if passes == 3:
                gl[rs, j:j+256] = l
            sm = jnp.sum(x, axis=1, keepdims=True)
            tot = sm if tot is None else tot + sm
        g1[rs, :] = jnp.broadcast_to(tot, (RT, B))
    nch = cols // CT
    bc = CT // B
    def copies(c, slot):
        return [pltpu.make_async_copy(stage.at[slot, :, pl.ds(u * B, B)], out_ref.at[:, c * bc + u, 0, :], sem.at[slot]) for u in range(bc)]
    def chunk(c, _):
        slot = lax.rem(c, 2)
        c0 = pl.multiple_of(c * CT, CT)
        zc = zc_ref[:, pl.ds(c0, CT)]
        x = zc.astype(f32)
        hc = jnp.sum(x * x, axis=0, keepdims=True) * cs
        kc = jnp.exp2(dot(zlt[...], zc) * (2 * cs) - wide(hlc[...], CT) - hc)
        mu = jnp.mean(kc, axis=0, keepdims=True)
        dh, dl = split(kc - mu)
        @pl.when(c >= 2)
        def _():
            for cp in copies(c, slot): cp.wait()
        for i in range(0, rows, RT):
            rs = slice(i, i + RT)
            t = dot(zrt[rs, :], zc) * (2 * cs) - wide(hr[rs, :], CT) - hc
            k = jnp.exp2(t)
            s = dot(gh[rs, :], dh)
            if passes == 3:
                s = s + dot(gh[rs, :], dl) + dot(gl[rs, :], dh)
            k = k - s - wide(g1[rs, :], CT) * mu
            stage[slot, rs, :] = k
        for u in range(bc):
            gb = (c * bc + u) * ncol + q
            a = gb // nrow
            @pl.when((gb % nrow == p))
            def _():
                r0 = pl.multiple_of(a * B, B)
                ri = lax.broadcasted_iota(jnp.int32, (B, B), 0)
                ci = lax.broadcasted_iota(jnp.int32, (B, B), 1)
                nzv = nz_ref[:, pl.ds(pl.multiple_of(gb * B, B), B)]
                stage[slot, pl.ds(r0, B), u*B:(u+1)*B] = stage[slot, pl.ds(r0, B), u*B:(u+1)*B] + jnp.where(ri == ci, jnp.broadcast_to(nzv, (B, B)), 0.0)
            @pl.when(gb * B < lead)
            def _():
                stage[slot, :, u*B:(u+1)*B] = jnp.zeros((rows, B), f32)
        @pl.when(p * B < lead)
        def _():
            stage[slot, :B, :] = jnp.zeros((B, CT), f32)
        for cp in copies(c, slot): cp.start()
        return 0
    lax.fori_loop(0, nch, chunk, 0)
    for c in (nch - 2, nch - 1):
        for cp in copies(c, c % 2): cp.wait()

def main_call(pos, zl, zr, zc, w, wt, nz, nrow=16, ncol=8, passes=3):
    width, lead = zl.shape; rows = zr.shape[1]; cols = zc.shape[1]
    V = pl.BlockSpec(memory_space=pltpu.VMEM)
    return pl.pallas_call(functools.partial(main_body, width=width, lead=lead, nrow=nrow, ncol=ncol, passes=passes),
        out_shape=(jax.ShapeDtypeStruct((rows, cols // B, 1, B), f32), jax.ShapeDtypeStruct((rows, B), f32)),
        in_specs=[pl.BlockSpec(memory_space=pltpu.SMEM)] + [V] * 6,
        out_specs=(pl.BlockSpec(memory_space=pltpu.HBM), V),
        scratch_shapes=[pltpu.VMEM((lead, width), bf16), pltpu.VMEM((rows, width), bf16)] +
          [pltpu.VMEM((rows, lead), bf16)] * 6 + [pltpu.VMEM((rows, B), f32)] * 2 + [pltpu.VMEM((lead, B), f32),
          pltpu.VMEM((2, rows, 256), f32), pltpu.SemaphoreType.DMA((2,))],
        compiler_params=pltpu.CompilerParams(vmem_limit_bytes=61*2**20),
    )(pos, zl, zr, zc, w, wt, nz)


def body(embeddings, inv_scale, noise):
    nrow = lax.axis_size("row")
    ncol = lax.axis_size("col")
    prow = lax.axis_index("row")
    qcol = lax.axis_index("col")
    total, fdev = embeddings.shape
    width = inv_scale.shape[0]
    crow = total // (TILE * nrow)
    ccol = total // (TILE * ncol)
    lead = PANELS * PB
    scale_part = lax.dynamic_slice_in_dim(inv_scale, (prow * ncol + qcol) * fdev, fdev)
    scaled = (embeddings.T.astype(jnp.float32) * scale_part[:, None]).astype(jnp.bfloat16)
    zl = lax.all_gather(scaled[:, :lead], ("row", "col"), axis=0, tiled=True)
    by_row = scaled.reshape(fdev, crow, nrow, TILE).transpose(2, 0, 1, 3).reshape(nrow, fdev, crow * TILE)
    by_col = scaled.reshape(fdev, ccol, ncol, TILE).transpose(2, 0, 1, 3).reshape(ncol, fdev, ccol * TILE)
    col_mine = lax.all_to_all(by_col, "col", split_axis=0, concat_axis=0, tiled=True)
    row_mine = lax.all_to_all(by_row, "row", split_axis=0, concat_axis=0, tiled=True)
    zc = lax.all_gather(col_mine, "row", axis=0, tiled=False).reshape(width, ccol * TILE)
    zr = lax.all_gather(row_mine, "col", axis=0, tiled=False).transpose(1, 0, 2, 3).reshape(width, crow * TILE)
    nz = noise[None]
    w, wt = chol_call(zl, nz[:, :lead])
    pos = jnp.stack([prow, qcol]).astype(jnp.int32)
    schur, factor = main_call(pos, zl, zr, zc, w, wt, nz, nrow=nrow, ncol=ncol, passes=3)
    return (
        factor.reshape(crow, 1, TILE, TILE),
        schur.reshape(crow, 1, TILE, ccol, 1, TILE),
    )


def solution(mesh):
    placed = (P(None, ("row", "col")), P(), P())
    return jax.shard_map(
        body,
        mesh=mesh,
        in_specs=placed,
        out_specs=(P(None, "row", None, "col"), P(None, "row", None, None, "col", None)),
        check_vma=False,
    )
```

```python
import functools
import math

import jax
import jax.numpy as jnp
from jax import lax
from jax.experimental import pallas as pl
from jax.experimental.pallas import tpu as pltpu
from jax.sharding import PartitionSpec as P

TILE = 128
PB = 512
PANELS = 2
PASSES = 3
B=128
def factor_block(load, store):
    lane = lax.broadcasted_iota(jnp.int32, (8, B), 1)
    sub = lax.broadcasted_iota(jnp.int32, (8, B), 0)
    X = [load(g) for g in range(B // 8)]
    for g in range(B // 8):
        P = X[g]
        base = 8 * g
        c = [jnp.broadcast_to(P[:, base + j:base + j + 1], (8, B)) for j in range(8)]
        s = [[jnp.broadcast_to(c[j][i:i + 1, :], (8, B)) if j <= i else None for j in range(8)] for i in range(8)]
        ingroup = (lane >= base) & (lane < base + 8)
        Pp = jnp.where(ingroup, jnp.where(lane - base == sub, 1.0, 0.0), P)
        r = [jnp.broadcast_to(Pp[k:k + 1, :], (8, B)) for k in range(8)]
        l = [[None] * 8 for _ in range(8)]
        dinv = [None] * 8
        for k in range(8):
            dinv[k] = 1.0 / s[k][k]
            for i in range(k + 1, 8):
                l[i][k] = s[i][k] * dinv[k]
                for j in range(k + 1, i + 1):
                    s[i][j] = s[i][j] - l[i][k] * s[j][k]
        f = []
        for k in range(8):
            v = r[k]
            for m in range(k):
                v = v - l[k][m] * f[m]
            f.append(v)
        w = [None] * 8
        for k in range(7, -1, -1):
            v = f[k] * dinv[k]
            for m in range(k + 1, 8):
                v = v - l[m][k] * w[m]
            w[k] = v
        fo, so = f[0], s[0][0]
        for k in range(1, 8):
            fo = jnp.where(sub == k, f[k], fo)
            so = jnp.where(sub == k, s[k][k], so)
        store(g, fo * lax.rsqrt(so))
        for i in range(g + 1, B // 8):
            Xi = X[i]
            acc = jnp.where(ingroup, 0.0, Xi)
            for k in range(8):
                acc = acc - jnp.broadcast_to(Xi[:, base + k:base + k + 1], (8, B)) * w[k]
            X[i] = acc

def split(x):
    hi = x.astype(jnp.bfloat16)
    return hi, (x - hi.astype(jnp.float32)).astype(jnp.bfloat16)

def dot(a, b):
    return jnp.dot(a, b, preferred_element_type=jnp.float32)

def dot3(a, b):
    ah, al = a; bh, bl = b
    return dot(ah, bh) + dot(ah, bl) + dot(al, bh)

LOG2E = math.log2(math.e)

def chol_body(zl_ref, noise_ref, w_ref, wt_ref, X, V, zt, n, width, poll=None):
    nb = n // B
    zt[...] = zl_ref[...].T
    zf = zl_ref[...].astype(jnp.float32)
    hc = jnp.sum(zf * zf, axis=0, keepdims=True) * (LOG2E / (2 * width))
    hcol = jnp.broadcast_to(hc, (8, n)).T[:, 0:1]
    for i in range(nb):
        rows = slice(i * B, (i + 1) * B)
        t = dot(zt[rows, :], zl_ref[...]) * (LOG2E / width) - hcol[rows, :] - hc
        k = jnp.exp2(t)
        ri = lax.broadcasted_iota(jnp.int32, (B, n), 0) + i * B
        ci = lax.broadcasted_iota(jnp.int32, (B, n), 1)
        X[rows, :] = k + jnp.where(ri == ci, jnp.broadcast_to(noise_ref[...], (B, n)), 0.0)
    tri = lax.broadcasted_iota(jnp.int32, (B, B), 0) >= lax.broadcasted_iota(jnp.int32, (B, B), 1)
    eye = jnp.where(lax.broadcasted_iota(jnp.int32, (B, B), 0) == lax.broadcasted_iota(jnp.int32, (B, B), 1), 1.0, 0.0)

    def step(b, _):
        if poll is not None:
            poll(b)
        r0 = pl.multiple_of(b * B, B)
        def load(g):
            return X[pl.ds(r0 + 8 * g, 8), pl.ds(r0, B)]
        def store(g, v):
            V[pl.ds(8 * g, 8), :] = v
        factor_block(load, store)
        v = jnp.where(tri, V[...], 0.0)
        X[pl.ds(r0, B), pl.ds(r0, B)] = eye
        P = dot3(split(v), split(X[pl.ds(r0, B), :]))
        X[pl.ds(r0, B), :] = P
        Ps = split(P)
        def upd(i, _):
            i0 = pl.multiple_of(i * B, B)
            T = X[pl.ds(r0, B), pl.ds(i0, B)].T
            X[pl.ds(i0, B), pl.ds(r0, B)] = jnp.zeros((B, B), jnp.float32)
            X[pl.ds(i0, B), :] = X[pl.ds(i0, B), :] - dot3(split(T), Ps)
            return 0
        lax.fori_loop(b + 1, nb, upd, 0)
        return 0
    lax.fori_loop(0, nb, step, 0)
    for i in range(nb):
        rows = slice(i * B, (i + 1) * B)
        ri = lax.broadcasted_iota(jnp.int32, (B, n), 0) + i * B
        ci = lax.broadcasted_iota(jnp.int32, (B, n), 1)
        w = jnp.where(ri >= ci, X[rows, :], 0.0)
        h, lo = split(w)
        w_ref[0, rows, :] = h; w_ref[1, rows, :] = lo
        wt_ref[0, :, rows] = h.T; wt_ref[1, :, rows] = lo.T


B=128
bf16=jnp.bfloat16; f32=jnp.float32

MESH = pl.DeviceIdType.MESH
HALF = 768


def lead_kernel(slab_ref, scale_ref, noise_ref, zl_out, zr_ref, zc_ref, w_ref, wt_ref,
                xs, xr, s16, zlb, zlo, X, V, zt, own_sem, ssem, rsem, *, width, lead, half):
    p = lax.axis_index("row")
    qq = lax.axis_index("col")
    z = qq // 2
    c = qq % 2
    y = p // 4
    x = p % 4
    k16 = pl.multiple_of((p * 4 + z) * 16, 16)
    nh = 16 * half

    def dev(pp, zz, cc):
        return (pp, zz * 2 + cc)

    def rot(v, d):
        return (v + d + 4) % 4

    def plane(dy, dx):
        return rot(y, dy) * 4 + rot(x, dx)

    plane_offsets = [(dy, dx) for dy in range(4) for dx in range(4) if (dy, dx) != (0, 0)]
    col_offsets = [(dz, dc) for dz in range(4) for dc in range(2) if (dz, dc) != (0, 0)]

    barrier = pltpu.get_barrier_semaphore()
    for dy, dx in plane_offsets:
        pl.semaphore_signal(barrier, inc=1, device_id=dev(plane(dy, dx), z, c), device_id_type=MESH)
    for dz, dc in col_offsets:
        pl.semaphore_signal(barrier, inc=1, device_id=dev(p, rot(z, dz), (c + dc) % 2), device_id_type=MESH)

    def remote(src, dst, i, target):
        return pltpu.make_async_remote_copy(src_ref=src, dst_ref=dst, send_sem=ssem.at[i], recv_sem=rsem.at[i],
                                            device_id=target, device_id_type=MESH)

    def step_a(pp, d):
        yy, xx = pp // 4, pp % 4
        return (yy * 4 + rot(xx, d)) * (1 - c) + (rot(yy, d) * 4 + xx) * c

    def step_b(pp, d):
        yy, xx = pp // 4, pp % 4
        return (yy * 4 + rot(xx, d)) * c + (rot(yy, d) * 4 + xx) * (1 - c)

    def block(pp):
        return pl.ds(pl.multiple_of(pp * 64, 64), 64)

    base = {}
    at = 0
    for name, n in (("X", 1), ("L1", 3), ("L2", 15), ("L3", 1), ("CA", 7), ("RA", 15), ("A1", 2), ("A2", 2),
                    ("B1", 8), ("B2", 8), ("Z1", 2), ("Z2", 2), ("PR", 1)):
        base[name] = at
        at += n
    DS = (0, 1, -1, 2)

    def exchange():
        return [remote(xs, xr, base["X"], dev(p, z, 1 - c))]

    def lead_z():
        r = zlb.at[c, pl.ds(k16, 16), :]
        return [remote(r, r, base["L1"] + d - 1, dev(p, rot(z, d), c)) for d in (1, 2, 3)]

    def lead_plane():
        r = zlb.at[c, block(p), :]
        return [remote(r, r, base["L2"] + n, dev(plane(dy, dx), z, c)) for n, (dy, dx) in enumerate(plane_offsets)]

    def lead_partner():
        r = zlb.at[c]
        return [remote(r, r, base["L3"], dev(p, z, 1 - c))]

    def col_a2a():
        out = []
        for n, (dz, dc) in enumerate(col_offsets):
            zz, cc = rot(z, dz), (c + dc) % 2
            out.append(remote(s16.at[:, zz * 2 + cc], zc_ref.at[:, c, pl.ds(k16, 16), :], base["CA"] + n, dev(p, zz, cc)))
        return out

    def row_a2a():
        out = []
        for n, (dy, dx) in enumerate(plane_offsets):
            pp = plane(dy, dx)
            out.append(remote(s16.at[pp // 8, pp % 8], zr_ref.at[c, p, z], base["RA"] + n, dev(pp, z, c)))
        return out

    def own_copies():
        return [pltpu.make_async_copy(s16.at[:, qq], zc_ref.at[:, c, pl.ds(k16, 16), :], own_sem.at[0]),
                pltpu.make_async_copy(s16.at[p // 8, p % 8], zr_ref.at[c, p, z], own_sem.at[1])]

    def a1():
        r = zc_ref.at[:, :, block(p), :]
        return [remote(r, r, base["A1"], dev(step_a(p, 1), z, c)), remote(r, r, base["A1"] + 1, dev(step_a(p, -1), z, c))]

    def a2():
        f = zc_ref.at[0, :, block(step_a(p, -1)), :]
        g = zc_ref.at[1, :, block(step_a(p, 1)), :]
        return [remote(f, f, base["A2"], dev(step_a(p, 1), z, c)), remote(g, g, base["A2"] + 1, dev(step_a(p, -1), z, c))]

    def b1(n):
        r = zc_ref.at[:, :, block(step_a(p, DS[n])), :]
        return [remote(r, r, base["B1"] + 2 * n, dev(step_b(p, 1), z, c)),
                remote(r, r, base["B1"] + 2 * n + 1, dev(step_b(p, -1), z, c))]

    def b2(n):
        f = zc_ref.at[0, :, block(step_a(step_b(p, -1), DS[n])), :]
        g = zc_ref.at[1, :, block(step_a(step_b(p, 1), DS[n])), :]
        return [remote(f, f, base["B2"] + 2 * n, dev(step_b(p, 1), z, c)),
                remote(g, g, base["B2"] + 2 * n + 1, dev(step_b(p, -1), z, c))]

    def z1():
        r = zr_ref.at[c, :, z]
        return [remote(r, r, base["Z1"], dev(p, rot(z, 1), c)), remote(r, r, base["Z1"] + 1, dev(p, rot(z, -1), c))]

    def z2():
        f = zr_ref.at[c, 0:8, rot(z, -1)]
        g = zr_ref.at[c, 8:16, rot(z, 1)]
        return [remote(f, f, base["Z2"], dev(p, rot(z, 1), c)), remote(g, g, base["Z2"] + 1, dev(p, rot(z, -1), c))]

    def partner_rows():
        r = zr_ref.at[c]
        return [remote(r, r, base["PR"], dev(p, z, 1 - c))]

    def start(copies):
        for cp in copies:
            cp.start()

    def arrived(copies):
        for cp in copies:
            cp.wait_recv()

    scale = scale_ref[:, 0:1]

    def scaled(sl):
        return (slab_ref[:, sl].astype(f32) * scale).astype(bf16).astype(f32)

    CH = 2048
    for h in range(2):
        @pl.when(c == 1 - h)
        def _():
            for o in range(0, nh, CH):
                xs[:, o:o + CH] = scaled(slice(h * nh + o, h * nh + o + CH))
    xs[:, nh:] = scaled(slice(0, lead))
    pl.semaphore_wait(barrier, len(plane_offsets) + len(col_offsets))
    start(exchange())
    arrived(exchange())

    def pair(own, other):
        first = own * (1 - c).astype(f32) + other * c.astype(f32)
        second = other * (1 - c).astype(f32) + own * c.astype(f32)
        return jnp.concatenate([first, second], axis=0).astype(bf16)

    for j in range(lead // B // 2):
        for h in range(2):
            @pl.when(c == h)
            def _():
                o = (2 * j + h) * B
                zlb[h, pl.ds(k16, 16), j * B:(j + 1) * B] = pair(xs[:, nh + o:nh + o + B], xr[:, nh + o:nh + o + B])
    start(lead_z())
    for h in range(2):
        @pl.when(c == h)
        def _():
            for a in range(half // B):
                own = scaled(slice(h * nh + a * 2048, h * nh + (a + 1) * 2048))
                both = pair(own, xr[:, a * 2048:(a + 1) * 2048])
                for s in range(16):
                    s16[s // 8, s % 8, :, a * B:(a + 1) * B] = both[:, s * B:(s + 1) * B]
    arrived(lead_z())
    start(lead_plane())
    arrived(lead_plane())
    start(lead_partner())
    start(col_a2a())
    start(own_copies())
    start(row_a2a())
    arrived(lead_partner())

    for u in range(lead // B):
        zlo[:, u * B:(u + 1) * B] = zlb[u % 2, :, (u // 2) * B:(u // 2 + 1) * B]
    zl_copy = pltpu.make_async_copy(zlo, zl_out, own_sem.at[2])
    zl_copy.start()

    def poll(b):
        @pl.when(b == 0)
        def _():
            for cp in own_copies():
                cp.wait()
            arrived(col_a2a())
            start(a1())
            arrived(row_a2a())
            start(z1())

        @pl.when(b == 1)
        def _():
            start(b1(0))
            arrived(a1())
            start(a2())
            start(b1(1))
            start(b1(2))
            arrived(z1())
            start(z2())

        @pl.when(b == 2)
        def _():
            arrived(a2())
            start(b1(3))
            arrived(z2())
            start(partner_rows())

        @pl.when(b == 3)
        def _():
            arrived(b1(0))
            start(b2(0))

        @pl.when(b == 4)
        def _():
            for n in (1, 2, 3):
                arrived(b1(n))
                start(b2(n))

    chol_body(zlo, noise_ref, w_ref, wt_ref, X, V, zt, lead, width, poll)
    for n in range(4):
        arrived(b2(n))
    arrived(partner_rows())
    zl_copy.wait()
    sent = exchange() + lead_z() + lead_plane() + lead_partner() + col_a2a() + row_a2a() + a1() + a2() + z1() + z2() + partner_rows()
    for n in range(4):
        sent += b1(n) + b2(n)
    for cp in sent:
        cp.wait_send()


def lead_call(slab, scale, noise, lead, width):
    total = slab.shape[1]
    half = total // 32
    o = jax.ShapeDtypeStruct((2, lead, lead), bf16)
    vm = pl.BlockSpec(memory_space=pltpu.VMEM)
    hbm = pl.BlockSpec(memory_space=pltpu.HBM)
    nsem = 67
    return pl.pallas_call(
        functools.partial(lead_kernel, width=width, lead=lead, half=half),
        out_shape=(jax.ShapeDtypeStruct((width, lead), bf16), jax.ShapeDtypeStruct((2, 16, 4, 16, half), bf16),
                   jax.ShapeDtypeStruct((2, 2, width, half), bf16), o, o),
        in_specs=[vm] * 3,
        out_specs=[hbm, hbm, hbm, vm, vm],
        scratch_shapes=[pltpu.VMEM((8, 16 * half + lead), f32), pltpu.VMEM((8, 16 * half + lead), f32),
                        pltpu.VMEM((2, 8, 16, half), bf16), pltpu.VMEM((2, width, lead // 2), bf16),
                        pltpu.VMEM((width, lead), bf16), pltpu.VMEM((lead, lead), f32), pltpu.VMEM((B, B), f32),
                        pltpu.VMEM((lead, width), bf16), pltpu.SemaphoreType.DMA((3,)),
                        pltpu.SemaphoreType.DMA((nsem,)), pltpu.SemaphoreType.DMA((nsem,))],
        compiler_params=pltpu.CompilerParams(vmem_limit_bytes=60 * 2**20, collective_id=0, has_side_effects=True),
    )(slab, scale, noise)


def main_body(pos_ref, zl_ref, zr_ref, zc_ref, w_ref, wt_ref, nz_ref, out_ref, fac_ref,
              zlt, zrt, kh, kl, lh, ll, gh, gl, g1, hr, hlc, stage, sem, *, width, lead, nrow, ncol, passes, RT=512, CT=256):
    half = zr_ref.shape[2]; rows = 2 * half
    p = pos_ref[0]; q = pos_ref[1]
    cs = LOG2E / (2 * width)
    for i in range(0, lead, 256):
        zlt[i:i+256, :] = zl_ref[:, i:i+256].T
    def colsq(ref, sl):
        x = ref[:, sl].astype(f32)
        return jnp.sum(x * x, axis=0, keepdims=True) * cs
    def lanecol(v):
        return jnp.broadcast_to(jnp.broadcast_to(v, (8, v.shape[1])).T[:, 0:1], (v.shape[1], B))
    for i in range(0, rows, 256):
        part = zr_ref.at[i // half]
        o = i % half
        zrt[i:i+256, :] = part[:, o:o+256].T
        hr[i:i+256, :] = lanecol(colsq(part, slice(o, o+256)))
    for i in range(0, lead, 256):
        hlc[i:i+256, :] = lanecol(colsq(zl_ref, slice(i, i+256)))
    def wide(x, n):
        return jnp.concatenate([x] * (n // B), axis=1)
    for j in range(0, lead, 256):
        hl = colsq(zl_ref, slice(j, j + 256))
        for i in range(0, rows, RT):
            t = dot(zrt[i:i+RT, :], zl_ref[:, j:j+256]) * (2 * cs) - wide(hr[i:i+RT, :], 256) - hl
            k = jnp.exp2(t)
            if i == 0:
                ri = lax.broadcasted_iota(jnp.int32, (B, 256), 0) + p * B
                ci = lax.broadcasted_iota(jnp.int32, (B, 256), 1) + j
                nug = jnp.where(ri == ci, jnp.broadcast_to(nz_ref[:, j:j+256], (B, 256)), 0.0)
                k = jnp.concatenate([k[:B] + nug, k[B:]], axis=0)
            h, l = split(k)
            kh[i:i+RT, j:j+256] = h
            kl[i:i+RT, j:j+256] = l
    for j in range(0, lead, 256):
        e = j + 256
        for i in range(0, rows, RT):
            rs = slice(i, i + RT)
            x = dot(kh[rs, :e], wt_ref[0, :e, j:e]) + dot(kh[rs, :e], wt_ref[1, :e, j:e]) + dot(kl[rs, :e], wt_ref[0, :e, j:e])
            h, l = split(x)
            lh[rs, j:e] = h
            ll[rs, j:e] = l
            for hb in range(2):
                @pl.when(q == j // B + hb)
                def _():
                    y = x[:, hb * B:(hb + 1) * B]
                    if i == 0:
                        ri = lax.broadcasted_iota(jnp.int32, (B, B), 0) + p * B
                        ci = lax.broadcasted_iota(jnp.int32, (B, B), 1) + (j + hb * B)
                        y = jnp.concatenate([jnp.where(ri >= ci, y[:B], 0.0), y[B:]], axis=0)
                    fac_ref[rs, :] = y
    for i in range(0, rows, RT):
        rs = slice(i, i + RT)
        tot = None
        for j in range(0, lead, 256):
            x = dot(lh[rs, j:], w_ref[0, j:, j:j+256]) + dot(lh[rs, j:], w_ref[1, j:, j:j+256]) + dot(ll[rs, j:], w_ref[0, j:, j:j+256])
            h, l = split(x)
            gh[rs, j:j+256] = h
            if passes == 3:
                gl[rs, j:j+256] = l
            sm = jnp.sum(x, axis=1, keepdims=True)
            tot = sm if tot is None else tot + sm
        g1[rs, :] = jnp.broadcast_to(tot, (RT, B))
    nch = 4 * half // CT
    bc = CT // B
    per = half // CT
    def col_block(c, u):
        g = c // per
        return 2 * ((g % 2) * (half // B) + (c % per) * bc + u) + g // 2
    def copies(c, slot):
        return [pltpu.make_async_copy(stage.at[slot, :, pl.ds(u * B, B)], out_ref.at[:, col_block(c, u), 0, :], sem.at[slot]) for u in range(bc)]
    def chunk(c, _):
        slot = lax.rem(c, 2)
        c0 = pl.multiple_of((c % per) * CT, CT)
        zc = zc_ref[c // per, :, pl.ds(c0, CT)]
        x = zc.astype(f32)
        hc = jnp.sum(x * x, axis=0, keepdims=True) * cs
        kc = jnp.exp2(dot(zlt[...], zc) * (2 * cs) - wide(hlc[...], CT) - hc)
        mu = jnp.mean(kc, axis=0, keepdims=True)
        dh, dl = split(kc - mu)
        @pl.when(c >= 2)
        def _():
            for cp in copies(c, slot): cp.wait()
        for i in range(0, rows, RT):
            rs = slice(i, i + RT)
            t = dot(zrt[rs, :], zc) * (2 * cs) - wide(hr[rs, :], CT) - hc
            k = jnp.exp2(t)
            s = dot(gh[rs, :], dh)
            if passes == 3:
                s = s + dot(gh[rs, :], dl) + dot(gl[rs, :], dh)
            k = k - s - wide(g1[rs, :], CT) * mu
            stage[slot, rs, :] = k
        for u in range(bc):
            gb = col_block(c, u) * ncol + q
            a = gb // nrow
            @pl.when((gb % nrow == p))
            def _():
                r0 = pl.multiple_of(a * B, B)
                ri = lax.broadcasted_iota(jnp.int32, (B, B), 0)
                ci = lax.broadcasted_iota(jnp.int32, (B, B), 1)
                nzv = nz_ref[:, pl.ds(pl.multiple_of(gb * B, B), B)]
                stage[slot, pl.ds(r0, B), u*B:(u+1)*B] = stage[slot, pl.ds(r0, B), u*B:(u+1)*B] + jnp.where(ri == ci, jnp.broadcast_to(nzv, (B, B)), 0.0)
            @pl.when(gb * B < lead)
            def _():
                stage[slot, :, u*B:(u+1)*B] = jnp.zeros((rows, B), f32)
        @pl.when(p * B < lead)
        def _():
            stage[slot, :B, :] = jnp.zeros((B, CT), f32)
        for cp in copies(c, slot): cp.start()
        return 0
    lax.fori_loop(0, nch, chunk, 0)
    for c in (nch - 2, nch - 1):
        for cp in copies(c, c % 2): cp.wait()

def main_call(pos, zl, zr, zc, w, wt, nz, nrow=16, ncol=8, passes=3):
    width, lead = zl.shape; rows = 2 * zr.shape[2]; cols = 4 * zc.shape[2]
    V = pl.BlockSpec(memory_space=pltpu.VMEM)
    return pl.pallas_call(functools.partial(main_body, width=width, lead=lead, nrow=nrow, ncol=ncol, passes=passes),
        out_shape=(jax.ShapeDtypeStruct((rows, cols // B, 1, B), f32), jax.ShapeDtypeStruct((rows, B), f32)),
        in_specs=[pl.BlockSpec(memory_space=pltpu.SMEM)] + [V] * 6,
        out_specs=(pl.BlockSpec(memory_space=pltpu.HBM), V),
        scratch_shapes=[pltpu.VMEM((lead, width), bf16), pltpu.VMEM((rows, width), bf16)] +
          [pltpu.VMEM((rows, lead), bf16)] * 6 + [pltpu.VMEM((rows, B), f32)] * 2 + [pltpu.VMEM((lead, B), f32),
          pltpu.VMEM((2, rows, 256), f32), pltpu.SemaphoreType.DMA((2,))],
        compiler_params=pltpu.CompilerParams(vmem_limit_bytes=61*2**20),
    )(pos, zl, zr, zc, w, wt, nz)


def body(embeddings, inv_scale, noise):
    nrow = lax.axis_size("row")
    ncol = lax.axis_size("col")
    prow = lax.axis_index("row")
    qcol = lax.axis_index("col")
    total, fdev = embeddings.shape
    width = inv_scale.shape[0]
    crow = total // (TILE * nrow)
    ccol = total // (TILE * ncol)
    lead = PANELS * PB
    scale_part = lax.dynamic_slice_in_dim(inv_scale, (prow * ncol + qcol) * fdev, fdev)
    scale = jnp.broadcast_to(scale_part[:, None], (fdev, TILE))
    nz = noise[None]
    zl, zr, zc, w, wt = lead_call(embeddings.T, scale, nz[:, :lead], lead, width)
    half = zr.shape[-1]
    pos = jnp.stack([prow, qcol]).astype(jnp.int32)
    schur, factor = main_call(pos, zl, zr.reshape(2, width, half), zc.reshape(4, width, half), w, wt, nz,
                              nrow=nrow, ncol=ncol, passes=PASSES)
    return (
        factor.reshape(crow, 1, TILE, TILE),
        schur.reshape(crow, 1, TILE, ccol, 1, TILE),
    )


def solution(mesh):
    placed = (P(None, ("row", "col")), P(), P())
    return jax.shard_map(
        body,
        mesh=mesh,
        in_specs=placed,
        out_specs=(P(None, "row", None, "col"), P(None, "row", None, None, "col", None)),
        check_vma=False,
    )
```

```python
import functools
import math

import jax
import jax.numpy as jnp
from jax import lax
from jax.experimental import pallas as pl
from jax.experimental.pallas import tpu as pltpu
from jax.sharding import PartitionSpec as P

TILE = 128
PB = 512
PANELS = 2
B=128
def factor_block(load, store, look=2):
    lane = lax.broadcasted_iota(jnp.int32, (8, B), 1)
    sub = lax.broadcasted_iota(jnp.int32, (8, B), 0)
    G = B // 8
    X = [load(g) for g in range(G)]

    def across(v, j):
        return jnp.broadcast_to(v[:, j:j + 1], (8, B))

    def down(v, i):
        return jnp.broadcast_to(v[i:i + 1, :], (8, B))

    def rcp(d):
        r0 = pl.reciprocal(d, approx=True)
        return r0 * (2.0 - d * r0)

    for g in range(G):
        P = X[g]
        base = 8 * g
        c = [across(P, base + j) for j in range(8)]
        s = [[down(c[j], i) if j <= i else None for j in range(8)] for i in range(8)]
        ingroup = (lane >= base) & (lane < base + 8)
        Pp = jnp.where(ingroup, jnp.where(lane - base == sub, 1.0, 0.0), P)
        f = [down(Pp, k) for k in range(8)]
        near = g + 1 < G
        if near:
            nk = [across(X[g + 1], base + k) for k in range(8)]
            acc = jnp.where(ingroup, 0.0, X[g + 1])
        m = [[None] * 8 for _ in range(8)]
        h = [None] * 8
        out = [None] * 8
        for k in range(0, 8, 2):
            a, b, d = s[k][k], s[k + 1][k], s[k + 1][k + 1]
            det = a * d - b * b
            rd = rcp(det)
            for i in range(k + 2, 8):
                u0 = d * s[i][k] - b * s[i][k + 1]
                u1 = a * s[i][k + 1] - b * s[i][k]
                m[i][k] = u0 * rd
                m[i][k + 1] = u1 * rd
                for j in range(k + 2, i + 1):
                    s[i][j] = s[i][j] - (u0 * s[j][k] + u1 * s[j][k + 1]) * rd
            for i in range(k + 2, 8):
                f[i] = f[i] - (m[i][k] * f[k] + m[i][k + 1] * f[k + 1])
                if near:
                    nk[i] = nk[i] - (m[i][k] * nk[k] + m[i][k + 1] * nk[k + 1])
            h[k] = (d * f[k] - b * f[k + 1]) * rd
            h[k + 1] = (a * f[k + 1] - b * f[k]) * rd
            if near:
                acc = acc - (nk[k] * h[k] + nk[k + 1] * h[k + 1])
            ra = lax.rsqrt(a)
            ra2 = ra * ra
            out[k] = f[k] * ra
            out[k + 1] = (f[k + 1] - b * ra2 * f[k]) * lax.rsqrt(det * ra2)
        if near:
            X[g + 1] = acc
        fo = out[0]
        for k in range(1, 8):
            fo = jnp.where(sub == k, out[k], fo)
        store(g, fo)
        if g + 2 >= G:
            continue
        w = list(h)
        for k in range(4, -1, -2):
            for i in range(k + 2, 8):
                w[k] = w[k] - m[i][k] * w[i]
                w[k + 1] = w[k + 1] - m[i][k + 1] * w[i]
        for i in range(g + 2, min(g + 1 + look, G)):
            acc = jnp.where(ingroup, 0.0, X[i])
            for k in range(8):
                acc = acc - across(X[i], base + k) * w[k]
            X[i] = acc
        first = g + 1 + look
        if first >= G:
            continue
        w8 = w[0]
        for k in range(1, 8):
            w8 = jnp.where(sub == k, w[k], w8)
        parts = []
        if base:
            parts.append(jnp.zeros((base, B), jnp.float32))
        parts.append(w8)
        if base + 8 < B:
            parts.append(jnp.zeros((B - base - 8, B), jnp.float32))
        rh, rl = split(jnp.concatenate(parts, axis=0))
        rest = jnp.concatenate(X[first:], axis=0)
        inr = (lax.broadcasted_iota(jnp.int32, rest.shape, 1) >= base) & (lax.broadcasted_iota(jnp.int32, rest.shape, 1) < base + 8)
        lh, ll = split(jnp.where(inr, rest, 0.0))
        new = jnp.where(inr, 0.0, rest) - (dot(lh, rh) + dot(lh, rl) + dot(ll, rh))
        for i in range(first, G):
            X[i] = new[8 * (i - first):8 * (i - first) + 8]

def split(x):
    hi = x.astype(jnp.bfloat16)
    return hi, (x - hi.astype(jnp.float32)).astype(jnp.bfloat16)

def dot(a, b):
    return jnp.dot(a, b, preferred_element_type=jnp.float32)

def dot3(a, b):
    ah, al = a; bh, bl = b
    return dot(ah, bh) + dot(ah, bl) + dot(al, bh)

LOG2E = math.log2(math.e)

def chol_body(zl_ref, noise_ref, w_hbm, X, V, R, wst, zt, wsem, n, width, poll=None):
    D = 2 * B
    steps = n // D
    zf = zl_ref[...].astype(jnp.float32)
    hc = jnp.sum(zf * zf, axis=0, keepdims=True) * (LOG2E / (2 * width))
    hcol = jnp.broadcast_to(hc, (8, n)).T[:, 0:1]
    for i in range(steps):
        lo = i * D
        rows = slice(lo, lo + D)
        zt[rows, :] = zl_ref[:, rows].T
        t = dot(zt[rows, :], zl_ref[:, lo:]) * (LOG2E / width) - hcol[rows, :] - hc[:, lo:]
        k = jnp.exp2(t)
        ri = lax.broadcasted_iota(jnp.int32, (D, n - lo), 0)
        ci = lax.broadcasted_iota(jnp.int32, (D, n - lo), 1)
        X[rows, lo:] = k + jnp.where(ri == ci, jnp.broadcast_to(noise_ref[:, lo:], (D, n - lo)), 0.0)
    tri = lax.broadcasted_iota(jnp.int32, (B, B), 0) >= lax.broadcasted_iota(jnp.int32, (B, B), 1)
    eye = jnp.where(lax.broadcasted_iota(jnp.int32, (B, B), 0) == lax.broadcasted_iota(jnp.int32, (B, B), 1), 1.0, 0.0)

    def eliminate(r0):
        factor_block(lambda g: X[pl.ds(r0 + 8 * g, 8), pl.ds(r0, B)], lambda g, v: V.__setitem__((pl.ds(8 * g, 8), slice(None)), v))
        v = jnp.where(tri, V[...], 0.0)
        X[pl.ds(r0, B), pl.ds(r0, B)] = eye
        X[pl.ds(r0, B), :] = dot3(split(v), split(X[pl.ds(r0, B), :]))

    def step(t, _):
        r0 = pl.multiple_of(t * D, D)
        r1 = pl.multiple_of(t * D + B, B)
        if poll is not None:
            poll(2 * t)
        eliminate(r0)
        T = X[pl.ds(r0, B), pl.ds(r1, B)].T
        X[pl.ds(r1, B), pl.ds(r0, B)] = jnp.zeros((B, B), jnp.float32)
        X[pl.ds(r1, B), :] = X[pl.ds(r1, B), :] - dot3(split(T), split(X[pl.ds(r0, B), :]))
        if poll is not None:
            poll(2 * t + 1)
        eliminate(r1)
        both = X[pl.ds(r0, D), :]
        ri = lax.broadcasted_iota(jnp.int32, (D, n), 0) + r0
        ci = lax.broadcasted_iota(jnp.int32, (D, n), 1)
        h, l = split(jnp.where(ri >= ci, both, 0.0))
        wst[0, pl.ds(r0, D), :] = h
        wst[1, pl.ds(r0, D), :] = l
        pltpu.make_async_copy(wst.at[:, pl.ds(r0, D), :], w_hbm.at[:, pl.ds(r0, D), :], wsem.at[t]).start()
        h, l = split(both)
        R[0] = h
        R[1] = l
        R[:, 0:B, pl.ds(r1, B)] = jnp.zeros((2, B, B), jnp.bfloat16)

        def upd(i, _):
            i0 = pl.multiple_of(i * D, D)
            T = X[pl.ds(r0, D), pl.ds(i0, D)].T
            X[pl.ds(i0, D), pl.ds(r0, D)] = jnp.zeros((D, D), jnp.float32)
            X[pl.ds(i0, D), :] = X[pl.ds(i0, D), :] - dot3(split(T), (R[0], R[1]))
            return 0
        lax.fori_loop(t + 1, steps, upd, 0)
        return 0
    lax.fori_loop(0, steps, step, 0)

def chol_done(w_hbm, wst, wsem, n):
    D = 2 * B
    for t in range(n // D):
        pltpu.make_async_copy(wst.at[:, pl.ds(t * D, D), :], w_hbm.at[:, pl.ds(t * D, D), :], wsem.at[t]).wait()

def chol_scratch(n, width):
    return [pltpu.VMEM((n, n), jnp.float32), pltpu.VMEM((B, B), jnp.float32), pltpu.VMEM((2, 2 * B, n), jnp.bfloat16),
            pltpu.VMEM((2, n, n), jnp.bfloat16), pltpu.VMEM((n, width), jnp.bfloat16), pltpu.SemaphoreType.DMA((n // (2 * B),))]


B=128
bf16=jnp.bfloat16; f32=jnp.float32

def dot_nt(a, b):
    return lax.dot_general(a, b, (((1,), (1,)), ((), ())), preferred_element_type=f32)

MESH = pl.DeviceIdType.MESH
HALF = 768


def lead_kernel(slab_ref, scale_ref, noise_ref, zl_out, zr_ref, zc_ref, w_ref,
                xs, xr, s16, zlb, zlo, X, V, R, wst, zt, wsem, own_sem, ssem, rsem, *, width, lead, half):
    p = lax.axis_index("row")
    qq = lax.axis_index("col")
    z = qq // 2
    c = qq % 2
    y = p // 4
    x = p % 4
    k16 = pl.multiple_of((p * 4 + z) * 16, 16)
    nh = 16 * half

    def dev(pp, zz, cc):
        return (pp, zz * 2 + cc)

    def rot(v, d):
        return (v + d + 4) % 4

    def plane(dy, dx):
        return rot(y, dy) * 4 + rot(x, dx)

    plane_offsets = [(dy, dx) for dy in range(4) for dx in range(4) if (dy, dx) != (0, 0)]
    col_offsets = [(dz, dc) for dz in range(4) for dc in range(2) if (dz, dc) != (0, 0)]

    barrier = pltpu.get_barrier_semaphore()
    for dy, dx in plane_offsets:
        pl.semaphore_signal(barrier, inc=1, device_id=dev(plane(dy, dx), z, c), device_id_type=MESH)
    for dz, dc in col_offsets:
        pl.semaphore_signal(barrier, inc=1, device_id=dev(p, rot(z, dz), (c + dc) % 2), device_id_type=MESH)

    def remote(src, dst, i, target):
        return pltpu.make_async_remote_copy(src_ref=src, dst_ref=dst, send_sem=ssem.at[i], recv_sem=rsem.at[i],
                                            device_id=target, device_id_type=MESH)

    def step_a(pp, d):
        yy, xx = pp // 4, pp % 4
        return (yy * 4 + rot(xx, d)) * (1 - c) + (rot(yy, d) * 4 + xx) * c

    def step_b(pp, d):
        yy, xx = pp // 4, pp % 4
        return (yy * 4 + rot(xx, d)) * c + (rot(yy, d) * 4 + xx) * (1 - c)

    def block(pp):
        return pl.ds(pl.multiple_of(pp * 64, 64), 64)

    base = {}
    at = 0
    for name, n in (("X", 1), ("L1", 3), ("L2", 15), ("L3", 1), ("CA", 7), ("RA", 15), ("A1", 2), ("A2", 2),
                    ("B1", 8), ("B2", 8), ("Z1", 2), ("Z2", 2), ("PR", 1)):
        base[name] = at
        at += n
    DS = (0, 1, -1, 2)

    def exchange():
        return [remote(xs, xr, base["X"], dev(p, z, 1 - c))]

    def lead_z():
        r = zlb.at[c, pl.ds(k16, 16), :]
        return [remote(r, r, base["L1"] + d - 1, dev(p, rot(z, d), c)) for d in (1, 2, 3)]

    def lead_plane():
        r = zlb.at[c, block(p), :]
        return [remote(r, r, base["L2"] + n, dev(plane(dy, dx), z, c)) for n, (dy, dx) in enumerate(plane_offsets)]

    def lead_partner():
        r = zlb.at[c]
        return [remote(r, r, base["L3"], dev(p, z, 1 - c))]

    def col_a2a():
        out = []
        for n, (dz, dc) in enumerate(col_offsets):
            zz, cc = rot(z, dz), (c + dc) % 2
            out.append(remote(s16.at[:, zz * 2 + cc], zc_ref.at[:, c, pl.ds(k16, 16), :], base["CA"] + n, dev(p, zz, cc)))
        return out

    def row_a2a():
        out = []
        for n, (dy, dx) in enumerate(plane_offsets):
            pp = plane(dy, dx)
            out.append(remote(s16.at[pp // 8, pp % 8], zr_ref.at[c, p, z], base["RA"] + n, dev(pp, z, c)))
        return out

    def own_copies():
        return [pltpu.make_async_copy(s16.at[:, qq], zc_ref.at[:, c, pl.ds(k16, 16), :], own_sem.at[0]),
                pltpu.make_async_copy(s16.at[p // 8, p % 8], zr_ref.at[c, p, z], own_sem.at[1])]

    def a1():
        r = zc_ref.at[:, :, block(p), :]
        return [remote(r, r, base["A1"], dev(step_a(p, 1), z, c)), remote(r, r, base["A1"] + 1, dev(step_a(p, -1), z, c))]

    def a2():
        f = zc_ref.at[0, :, block(step_a(p, -1)), :]
        g = zc_ref.at[1, :, block(step_a(p, 1)), :]
        return [remote(f, f, base["A2"], dev(step_a(p, 1), z, c)), remote(g, g, base["A2"] + 1, dev(step_a(p, -1), z, c))]

    def b1(n):
        r = zc_ref.at[:, :, block(step_a(p, DS[n])), :]
        return [remote(r, r, base["B1"] + 2 * n, dev(step_b(p, 1), z, c)),
                remote(r, r, base["B1"] + 2 * n + 1, dev(step_b(p, -1), z, c))]

    def b2(n):
        f = zc_ref.at[0, :, block(step_a(step_b(p, -1), DS[n])), :]
        g = zc_ref.at[1, :, block(step_a(step_b(p, 1), DS[n])), :]
        return [remote(f, f, base["B2"] + 2 * n, dev(step_b(p, 1), z, c)),
                remote(g, g, base["B2"] + 2 * n + 1, dev(step_b(p, -1), z, c))]

    def z1():
        r = zr_ref.at[c, :, z]
        return [remote(r, r, base["Z1"], dev(p, rot(z, 1), c)), remote(r, r, base["Z1"] + 1, dev(p, rot(z, -1), c))]

    def z2():
        f = zr_ref.at[c, 0:8, rot(z, -1)]
        g = zr_ref.at[c, 8:16, rot(z, 1)]
        return [remote(f, f, base["Z2"], dev(p, rot(z, 1), c)), remote(g, g, base["Z2"] + 1, dev(p, rot(z, -1), c))]

    def partner_rows():
        r = zr_ref.at[c]
        return [remote(r, r, base["PR"], dev(p, z, 1 - c))]

    def start(copies):
        for cp in copies:
            cp.start()

    def arrived(copies):
        for cp in copies:
            cp.wait_recv()

    scale = scale_ref[:, 0:1]

    def scaled(sl):
        return (slab_ref[:, sl].astype(f32) * scale).astype(bf16).astype(f32)

    CH = 2048
    for h in range(2):
        @pl.when(c == 1 - h)
        def _():
            for o in range(0, nh, CH):
                xs[:, o:o + CH] = scaled(slice(h * nh + o, h * nh + o + CH))
    xs[:, nh:] = scaled(slice(0, lead))
    pl.semaphore_wait(barrier, len(plane_offsets) + len(col_offsets))
    start(exchange())
    arrived(exchange())

    def pair(own, other):
        first = own * (1 - c).astype(f32) + other * c.astype(f32)
        second = other * (1 - c).astype(f32) + own * c.astype(f32)
        return jnp.concatenate([first, second], axis=0).astype(bf16)

    for j in range(lead // B // 2):
        for h in range(2):
            @pl.when(c == h)
            def _():
                o = (2 * j + h) * B
                zlb[h, pl.ds(k16, 16), j * B:(j + 1) * B] = pair(xs[:, nh + o:nh + o + B], xr[:, nh + o:nh + o + B])
    start(lead_z())
    for h in range(2):
        @pl.when(c == h)
        def _():
            for a in range(half // B):
                own = scaled(slice(h * nh + a * 2048, h * nh + (a + 1) * 2048))
                both = pair(own, xr[:, a * 2048:(a + 1) * 2048])
                for s in range(16):
                    s16[s // 8, s % 8, :, a * B:(a + 1) * B] = both[:, s * B:(s + 1) * B]
    arrived(lead_z())
    start(lead_plane())
    arrived(lead_plane())
    start(lead_partner())
    start(col_a2a())
    start(own_copies())
    start(row_a2a())
    arrived(lead_partner())

    for u in range(lead // B):
        zlo[:, u * B:(u + 1) * B] = zlb[u % 2, :, (u // 2) * B:(u // 2 + 1) * B]
    zl_copy = pltpu.make_async_copy(zlo, zl_out, own_sem.at[2])
    zl_copy.start()

    def poll(b):
        @pl.when(b == 0)
        def _():
            for cp in own_copies():
                cp.wait()
            arrived(col_a2a())
            start(a1())
            arrived(row_a2a())
            start(z1())

        @pl.when(b == 1)
        def _():
            start(b1(0))

        @pl.when(b == 2)
        def _():
            arrived(a1())
            start(a2())
            start(b1(1))
            start(b1(2))
            arrived(z1())
            start(z2())

        @pl.when(b == 3)
        def _():
            arrived(a2())
            start(b1(3))

        @pl.when(b == 4)
        def _():
            arrived(z2())
            start(partner_rows())
            arrived(b1(0))
            start(b2(0))

        @pl.when(b == 5)
        def _():
            for n in (1, 2):
                arrived(b1(n))
                start(b2(n))

        @pl.when(b == 6)
        def _():
            arrived(b1(3))
            start(b2(3))

    chol_body(zlo, noise_ref, w_ref, X, V, R, wst, zt, wsem, lead, width, poll)
    for n in range(4):
        arrived(b2(n))
    arrived(partner_rows())
    zl_copy.wait()
    chol_done(w_ref, wst, wsem, lead)
    sent = exchange() + lead_z() + lead_plane() + lead_partner() + col_a2a() + row_a2a() + a1() + a2() + z1() + z2() + partner_rows()
    for n in range(4):
        sent += b1(n) + b2(n)
    for cp in sent:
        cp.wait_send()


def lead_call(slab, scale, noise, lead, width):
    total = slab.shape[1]
    half = total // 32
    o = jax.ShapeDtypeStruct((2, lead, lead), bf16)
    vm = pl.BlockSpec(memory_space=pltpu.VMEM)
    hbm = pl.BlockSpec(memory_space=pltpu.HBM)
    nsem = 67
    return pl.pallas_call(
        functools.partial(lead_kernel, width=width, lead=lead, half=half),
        out_shape=(jax.ShapeDtypeStruct((width, lead), bf16), jax.ShapeDtypeStruct((2, 16, 4, 16, half), bf16),
                   jax.ShapeDtypeStruct((2, 2, width, half), bf16), o),
        in_specs=[vm] * 3,
        out_specs=[hbm] * 4,
        scratch_shapes=[pltpu.VMEM((8, 16 * half + lead), f32), pltpu.VMEM((8, 16 * half + lead), f32),
                        pltpu.VMEM((2, 8, 16, half), bf16), pltpu.VMEM((2, width, lead // 2), bf16),
                        pltpu.VMEM((width, lead), bf16)] + chol_scratch(lead, width) + [pltpu.SemaphoreType.DMA((3,)),
                        pltpu.SemaphoreType.DMA((nsem,)), pltpu.SemaphoreType.DMA((nsem,))],
        compiler_params=pltpu.CompilerParams(vmem_limit_bytes=60 * 2**20, collective_id=0, has_side_effects=True),
    )(slab, scale, noise)


def main_body(pos_ref, limit_ref, zl_hbm, zr_hbm, zc_hbm, w_hbm, nz_ref, out_ref, fac_ref,
              zl_ref, zr_ref, zc_ref, w_ref, zlt, zrt, kh, kl, lh, ll, gh, gl, dh, mus, g1, hr, hlc, stage, isem, sem,
              *, width, lead, nrow, ncol, RT=512, CT=768):
    half = zr_ref.shape[2]; rows = 2 * half
    p = pos_ref[0]; q = pos_ref[1]
    cs = LOG2E / (2 * width)
    loads = [pltpu.make_async_copy(a, b, isem.at[n]) for n, (a, b) in enumerate(
        ((zl_hbm, zl_ref), (zr_hbm, zr_ref), (w_hbm, w_ref), (zc_hbm, zc_ref)))]
    for cp in loads:
        cp.start()
    loads[0].wait()
    for i in range(0, lead, 256):
        zlt[i:i+256, :] = zl_ref[:, i:i+256].T
    def colsq(ref, sl):
        x = ref[:, sl].astype(f32)
        return jnp.sum(x * x, axis=0, keepdims=True) * cs
    def lanecol(v):
        return jnp.broadcast_to(jnp.broadcast_to(v, (8, v.shape[1])).T[:, 0:1], (v.shape[1], B))
    for i in range(0, lead, 256):
        hlc[i:i+256, :] = lanecol(colsq(zl_ref, slice(i, i+256)))
    loads[1].wait()
    for i in range(0, rows, 256):
        part = zr_ref.at[i // half]
        o = i % half
        zrt[i:i+256, :] = part[:, o:o+256].T
        hr[i:i+256, :] = lanecol(colsq(part, slice(o, o+256)))
    def wide(x, n):
        return jnp.concatenate([x] * (n // B), axis=1)
    for j in range(0, lead, 256):
        hl = colsq(zl_ref, slice(j, j + 256))
        for i in range(0, rows, RT):
            t = dot(zrt[i:i+RT, :], zl_ref[:, j:j+256]) * (2 * cs) - wide(hr[i:i+RT, :], 256) - hl
            k = jnp.exp2(t)
            if i == 0:
                ri = lax.broadcasted_iota(jnp.int32, (B, 256), 0) + p * B
                ci = lax.broadcasted_iota(jnp.int32, (B, 256), 1) + j
                nug = jnp.where(ri == ci, jnp.broadcast_to(nz_ref[:, j:j+256], (B, 256)), 0.0)
                k = jnp.concatenate([k[:B] + nug, k[B:]], axis=0)
            h, l = split(k)
            kh[i:i+RT, j:j+256] = h
            kl[i:i+RT, j:j+256] = l
    loads[2].wait()
    for j in range(0, lead, 256):
        e = j + 256
        for i in range(0, rows, RT):
            rs = slice(i, i + RT)
            x = dot_nt(kh[rs, :e], w_ref[0, j:e, :e]) + dot_nt(kh[rs, :e], w_ref[1, j:e, :e]) + dot_nt(kl[rs, :e], w_ref[0, j:e, :e])
            h, l = split(x)
            lh[rs, j:e] = h
            ll[rs, j:e] = l
            for hb in range(2):
                @pl.when(q == j // B + hb)
                def _():
                    fac_ref[rs, :] = x[:, hb * B:(hb + 1) * B]
    @pl.when(p * B < lead)
    def _():
        ri = lax.broadcasted_iota(jnp.int32, (B, B), 0) + p * B
        ci = lax.broadcasted_iota(jnp.int32, (B, B), 1) + q * B
        fac_ref[:B, :] = jnp.where(ri >= ci, fac_ref[:B, :], 0.0)
    gsq = [None] * (lead // 256)
    for i in range(0, rows, RT):
        rs = slice(i, i + RT)
        tot = None
        for j in range(0, lead, 256):
            x = dot(lh[rs, j:], w_ref[0, j:, j:j+256]) + dot(lh[rs, j:], w_ref[1, j:, j:j+256]) + dot(ll[rs, j:], w_ref[0, j:, j:j+256])
            h, l = split(x)
            gh[rs, j:j+256] = h
            gl[rs, j:j+256] = l
            sm = jnp.sum(x, axis=1, keepdims=True)
            tot = sm if tot is None else tot + sm
            sq = jnp.sum(x * x, axis=0, keepdims=True)
            n = j // 256
            gsq[n] = sq if gsq[n] is None else gsq[n] + sq
        g1[rs, :] = jnp.broadcast_to(tot, (RT, B))
    gs = jnp.broadcast_to(jnp.concatenate(gsq, axis=1), (8, lead))
    loads[3].wait()
    nch = 4 * half // CT
    bc = CT // B
    per = half // CT
    def col_block(c, u):
        g = c // per
        return 2 * ((g % 2) * (half // B) + (c % per) * bc + u) + g // 2
    def copies(c, slot, i):
        return [pltpu.make_async_copy(stage.at[slot, pl.ds(i, RT), pl.ds(u * B, B)],
                                      out_ref.at[pl.ds(i, RT), col_block(c, u), 0, :], sem.at[slot, i // RT, u]) for u in range(bc)]
    LT = 256
    def finish(c, slot, i):
        for u in range(bc):
            gb = col_block(c, u) * ncol + q
            a = gb // nrow
            @pl.when((gb % nrow == p) & (a * B >= i) & (a * B < i + RT))
            def _():
                r0 = pl.multiple_of(a * B, B)
                ri = lax.broadcasted_iota(jnp.int32, (B, B), 0)
                ci = lax.broadcasted_iota(jnp.int32, (B, B), 1)
                nzv = nz_ref[:, pl.ds(pl.multiple_of(gb * B, B), B)]
                at = (slot, pl.ds(r0, B), slice(u*B, (u+1)*B))
                stage[at] = stage[at] + jnp.where(ri == ci, jnp.broadcast_to(nzv, (B, B)), 0.0)
            @pl.when(gb * B < lead)
            def _():
                stage[slot, i:i+RT, u*B:(u+1)*B] = jnp.zeros((RT, B), f32)
        if i == 0:
            @pl.when(p * B < lead)
            def _():
                stage[slot, :B, :] = jnp.zeros((B, CT), f32)
        for cp in copies(c, slot, i): cp.start()

    def chunk(c, _):
        slot = lax.rem(c, 2)
        c0 = pl.multiple_of((c % per) * CT, CT)
        zc = zc_ref[c // per, :, pl.ds(c0, CT)]
        x = zc.astype(f32)
        hc = jnp.sum(x * x, axis=0, keepdims=True) * cs
        mu = None
        gd = None
        for i in range(0, lead, LT):
            kc = jnp.exp2(dot(zlt[i:i+LT, :], zc) * (2 * cs) - wide(hlc[i:i+LT, :], CT) - hc)
            if mu is None:
                mu = jnp.mean(kc, axis=0, keepdims=True)
                mus[...] = jnp.broadcast_to(mu, (8, CT))
            dd = kc - mu
            dh[i:i+LT, :] = dd.astype(bf16)
            d2 = dd * dd
            ds = d2[:, :B]
            for u in range(1, bc):
                ds = ds + d2[:, u*B:(u+1)*B]
            part = dot(gs[:, i:i+LT], ds)
            gd = part if gd is None else gd + part
        err = jnp.sum(gd) * (1.0 / 8) * (2.0 * 2.0 ** -19)
        good = err <= limit_ref[0]
        @pl.when(c >= 2)
        def _():
            for i in range(0, rows, RT):
                for cp in copies(c, slot, i): cp.wait()
        @pl.when(good)
        def _():
            for i in range(0, rows, RT):
                rs = slice(i, i + RT)
                k = jnp.exp2(dot(zrt[rs, :], zc) * (2 * cs) - wide(hr[rs, :], CT) - hc)
                stage[slot, rs, :] = k - dot(gh[rs, :], dh[...]) - wide(g1[rs, :], CT) * mu
                finish(c, slot, i)
        @pl.when(jnp.logical_not(good))
        def _():
            def rowtile(n, _):
                rs = pl.ds(pl.multiple_of(n * 256, 256), 256)
                k = jnp.exp2(dot(zrt[rs, :], zc) * (2 * cs) - wide(hr[rs, :], CT) - hc)
                stage[slot, rs, :] = k - wide(g1[rs, :], CT) * mu
                return 0
            lax.fori_loop(0, rows // 256, rowtile, 0)
            def leadtile(m, _):
                ls = pl.ds(pl.multiple_of(m * LT, LT), LT)
                dd = jnp.exp2(dot(zlt[ls, :], zc) * (2 * cs) - wide(hlc[ls, :], CT) - hc) - mus[0:1, :]
                h, l = split(dd)
                def rt(n, _):
                    rs = pl.ds(pl.multiple_of(n * 256, 256), 256)
                    stage[slot, rs, :] = stage[slot, rs, :] - (dot(gh[rs, ls], h) + dot(gh[rs, ls], l) + dot(gl[rs, ls], h))
                    return 0
                lax.fori_loop(0, rows // 256, rt, 0)
                return 0
            lax.fori_loop(0, lead // LT, leadtile, 0)
            for i in range(0, rows, RT):
                finish(c, slot, i)
        return 0
    lax.fori_loop(0, nch, chunk, 0)
    for c in (nch - 2, nch - 1):
        for i in range(0, rows, RT):
            for cp in copies(c, c % 2, i): cp.wait()

def main_call(pos, limit, zl, zr, zc, w, nz, nrow=16, ncol=8):
    width, lead = zl.shape; half = zr.shape[2]; rows = 2 * half; cols = 4 * half
    V = pl.BlockSpec(memory_space=pltpu.VMEM)
    H = pl.BlockSpec(memory_space=pltpu.HBM)
    S = pl.BlockSpec(memory_space=pltpu.SMEM)
    CT = 768
    return pl.pallas_call(functools.partial(main_body, width=width, lead=lead, nrow=nrow, ncol=ncol, CT=CT),
        out_shape=(jax.ShapeDtypeStruct((rows, cols // B, 1, B), f32), jax.ShapeDtypeStruct((rows, B), f32)),
        in_specs=[S, S, H, H, H, H, V],
        out_specs=(H, V),
        scratch_shapes=[pltpu.VMEM(zl.shape, bf16), pltpu.VMEM(zr.shape, bf16), pltpu.VMEM(zc.shape, bf16), pltpu.VMEM(w.shape, bf16),
          pltpu.VMEM((lead, width), bf16), pltpu.VMEM((rows, width), bf16)] +
          [pltpu.VMEM((rows, lead), bf16)] * 6 + [pltpu.VMEM((lead, CT), bf16), pltpu.VMEM((8, CT), f32)] +
          [pltpu.VMEM((rows, B), f32)] * 2 + [pltpu.VMEM((lead, B), f32),
          pltpu.VMEM((2, rows, CT), f32), pltpu.SemaphoreType.DMA((4,)), pltpu.SemaphoreType.DMA((2, 3, CT // B))],
        compiler_params=pltpu.CompilerParams(vmem_limit_bytes=61*2**20),
    )(pos, limit, zl, zr, zc, w, nz)


CHUNK = 768


def body(embeddings, inv_scale, noise):
    nrow = lax.axis_size("row")
    ncol = lax.axis_size("col")
    prow = lax.axis_index("row")
    qcol = lax.axis_index("col")
    total, fdev = embeddings.shape
    width = inv_scale.shape[0]
    crow = total // (TILE * nrow)
    ccol = total // (TILE * ncol)
    lead = PANELS * PB
    scale_part = lax.dynamic_slice_in_dim(inv_scale, (prow * ncol + qcol) * fdev, fdev)
    scale = jnp.broadcast_to(scale_part[:, None], (fdev, TILE))
    nz = noise[None]
    zl, zr, zc, w = lead_call(embeddings.T, scale, nz[:, :lead], lead, width)
    half = zr.shape[-1]
    pos = jnp.stack([prow, qcol]).astype(jnp.int32)
    limit = (jnp.mean(noise * noise) * (0.0018 ** 2 / total * (crow * TILE) * CHUNK)).reshape(1)
    schur, factor = main_call(pos, limit, zl, zr.reshape(2, width, half), zc.reshape(4, width, half), w, nz,
                              nrow=nrow, ncol=ncol)
    return (
        factor.reshape(crow, 1, TILE, TILE),
        schur.reshape(crow, 1, TILE, ccol, 1, TILE),
    )


def solution(mesh):
    placed = (P(None, ("row", "col")), P(), P())
    return jax.shard_map(
        body,
        mesh=mesh,
        in_specs=placed,
        out_specs=(P(None, "row", None, "col"), P(None, "row", None, None, "col", None)),
        check_vma=False,
    )
```

```python
import functools
import math

import jax
import jax.numpy as jnp
from jax import lax
from jax.experimental import pallas as pl
from jax.experimental.pallas import tpu as pltpu
from jax.sharding import PartitionSpec as P

TILE = 128
PB = 512
PANELS = 2
B=128
def factor_block(load, store, look=2):
    lane = lax.broadcasted_iota(jnp.int32, (8, B), 1)
    sub = lax.broadcasted_iota(jnp.int32, (8, B), 0)
    G = B // 8
    X = [load(g) for g in range(G)]

    def across(v, j):
        return jnp.broadcast_to(v[:, j:j + 1], (8, B))

    def down(v, i):
        return jnp.broadcast_to(v[i:i + 1, :], (8, B))

    def rcp(d):
        r0 = pl.reciprocal(d, approx=True)
        return r0 * (2.0 - d * r0)

    for g in range(G):
        P = X[g]
        base = 8 * g
        c = [across(P, base + j) for j in range(8)]
        s = [[down(c[j], i) if j <= i else None for j in range(8)] for i in range(8)]
        ingroup = (lane >= base) & (lane < base + 8)
        Pp = jnp.where(ingroup, jnp.where(lane - base == sub, 1.0, 0.0), P)
        f = [down(Pp, k) for k in range(8)]
        near = g + 1 < G
        if near:
            nk = [across(X[g + 1], base + k) for k in range(8)]
            acc = jnp.where(ingroup, 0.0, X[g + 1])
        m = [[None] * 8 for _ in range(8)]
        h = [None] * 8
        out = [None] * 8
        for k in range(0, 8, 2):
            a, b, d = s[k][k], s[k + 1][k], s[k + 1][k + 1]
            det = a * d - b * b
            rd = rcp(det)
            for i in range(k + 2, 8):
                u0 = d * s[i][k] - b * s[i][k + 1]
                u1 = a * s[i][k + 1] - b * s[i][k]
                m[i][k] = u0 * rd
                m[i][k + 1] = u1 * rd
                for j in range(k + 2, i + 1):
                    s[i][j] = s[i][j] - (u0 * s[j][k] + u1 * s[j][k + 1]) * rd
            for i in range(k + 2, 8):
                f[i] = f[i] - (m[i][k] * f[k] + m[i][k + 1] * f[k + 1])
                if near:
                    nk[i] = nk[i] - (m[i][k] * nk[k] + m[i][k + 1] * nk[k + 1])
            h[k] = (d * f[k] - b * f[k + 1]) * rd
            h[k + 1] = (a * f[k + 1] - b * f[k]) * rd
            if near:
                acc = acc - (nk[k] * h[k] + nk[k + 1] * h[k + 1])
            ra = lax.rsqrt(a)
            ra2 = ra * ra
            out[k] = f[k] * ra
            out[k + 1] = (f[k + 1] - b * ra2 * f[k]) * lax.rsqrt(det * ra2)
        if near:
            X[g + 1] = acc
        fo = out[0]
        for k in range(1, 8):
            fo = jnp.where(sub == k, out[k], fo)
        store(g, fo)
        if g + 2 >= G:
            continue
        w = list(h)
        for k in range(4, -1, -2):
            for i in range(k + 2, 8):
                w[k] = w[k] - m[i][k] * w[i]
                w[k + 1] = w[k + 1] - m[i][k + 1] * w[i]
        for i in range(g + 2, min(g + 1 + look, G)):
            acc = jnp.where(ingroup, 0.0, X[i])
            for k in range(8):
                acc = acc - across(X[i], base + k) * w[k]
            X[i] = acc
        first = g + 1 + look
        if first >= G:
            continue
        w8 = w[0]
        for k in range(1, 8):
            w8 = jnp.where(sub == k, w[k], w8)
        parts = []
        if base:
            parts.append(jnp.zeros((base, B), jnp.float32))
        parts.append(w8)
        if base + 8 < B:
            parts.append(jnp.zeros((B - base - 8, B), jnp.float32))
        rh, rl = split(jnp.concatenate(parts, axis=0))
        rest = jnp.concatenate(X[first:], axis=0)
        inr = (lax.broadcasted_iota(jnp.int32, rest.shape, 1) >= base) & (lax.broadcasted_iota(jnp.int32, rest.shape, 1) < base + 8)
        lh, ll = split(jnp.where(inr, rest, 0.0))
        new = jnp.where(inr, 0.0, rest) - (dot(lh, rh) + dot(lh, rl) + dot(ll, rh))
        for i in range(first, G):
            X[i] = new[8 * (i - first):8 * (i - first) + 8]

def split(x):
    hi = x.astype(jnp.bfloat16)
    return hi, (x - hi.astype(jnp.float32)).astype(jnp.bfloat16)

def dot(a, b):
    return jnp.dot(a, b, preferred_element_type=jnp.float32)

def dot3(a, b):
    ah, al = a; bh, bl = b
    return dot(ah, bh) + dot(ah, bl) + dot(al, bh)

LOG2E = math.log2(math.e)

def chol_body(zl_ref, noise_ref, w_hbm, X, V, R, wst, zt, wsem, n, width, poll=None):
    D = 2 * B
    steps = n // D
    zf = zl_ref[...].astype(jnp.float32)
    hc = jnp.sum(zf * zf, axis=0, keepdims=True) * (LOG2E / (2 * width))
    hcol = jnp.broadcast_to(hc, (8, n)).T[:, 0:1]
    nzl = jnp.concatenate([noise_ref[i:i + 1, :] for i in range(n // B)], axis=1)
    for i in range(steps):
        lo = i * D
        rows = slice(lo, lo + D)
        zt[rows, :] = zl_ref[:, rows].T
        t = dot(zt[rows, :], zl_ref[:, lo:]) * (LOG2E / width) - hcol[rows, :] - hc[:, lo:]
        k = jnp.exp2(t)
        ri = lax.broadcasted_iota(jnp.int32, (D, n - lo), 0)
        ci = lax.broadcasted_iota(jnp.int32, (D, n - lo), 1)
        X[rows, lo:] = k + jnp.where(ri == ci, jnp.broadcast_to(nzl[:, lo:], (D, n - lo)), 0.0)
    tri = lax.broadcasted_iota(jnp.int32, (B, B), 0) >= lax.broadcasted_iota(jnp.int32, (B, B), 1)
    eye = jnp.where(lax.broadcasted_iota(jnp.int32, (B, B), 0) == lax.broadcasted_iota(jnp.int32, (B, B), 1), 1.0, 0.0)

    def eliminate(r0):
        factor_block(lambda g: X[pl.ds(r0 + 8 * g, 8), pl.ds(r0, B)], lambda g, v: V.__setitem__((pl.ds(8 * g, 8), slice(None)), v))
        v = jnp.where(tri, V[...], 0.0)
        X[pl.ds(r0, B), pl.ds(r0, B)] = eye
        X[pl.ds(r0, B), :] = dot3(split(v), split(X[pl.ds(r0, B), :]))

    def step(t, _):
        r0 = pl.multiple_of(t * D, D)
        r1 = pl.multiple_of(t * D + B, B)
        if poll is not None:
            poll(2 * t)
        eliminate(r0)
        T = X[pl.ds(r0, B), pl.ds(r1, B)].T
        X[pl.ds(r1, B), pl.ds(r0, B)] = jnp.zeros((B, B), jnp.float32)
        X[pl.ds(r1, B), :] = X[pl.ds(r1, B), :] - dot3(split(T), split(X[pl.ds(r0, B), :]))
        if poll is not None:
            poll(2 * t + 1)
        eliminate(r1)
        both = X[pl.ds(r0, D), :]
        ri = lax.broadcasted_iota(jnp.int32, (D, n), 0) + r0
        ci = lax.broadcasted_iota(jnp.int32, (D, n), 1)
        h, l = split(jnp.where(ri >= ci, both, 0.0))
        wst[0, pl.ds(r0, D), :] = h
        wst[1, pl.ds(r0, D), :] = l
        pltpu.make_async_copy(wst.at[:, pl.ds(r0, D), :], w_hbm.at[:, pl.ds(r0, D), :], wsem.at[t]).start()
        h, l = split(both)
        R[0] = h
        R[1] = l
        R[:, 0:B, pl.ds(r1, B)] = jnp.zeros((2, B, B), jnp.bfloat16)

        def upd(i, _):
            i0 = pl.multiple_of(i * D, D)
            T = X[pl.ds(r0, D), pl.ds(i0, D)].T
            X[pl.ds(i0, D), pl.ds(r0, D)] = jnp.zeros((D, D), jnp.float32)
            X[pl.ds(i0, D), :] = X[pl.ds(i0, D), :] - dot3(split(T), (R[0], R[1]))
            return 0
        lax.fori_loop(t + 1, steps, upd, 0)
        return 0
    lax.fori_loop(0, steps, step, 0)

def chol_done(w_hbm, wst, wsem, n):
    D = 2 * B
    for t in range(n // D):
        pltpu.make_async_copy(wst.at[:, pl.ds(t * D, D), :], w_hbm.at[:, pl.ds(t * D, D), :], wsem.at[t]).wait()

def chol_scratch(n, width):
    return [pltpu.VMEM((n, n), jnp.float32), pltpu.VMEM((B, B), jnp.float32), pltpu.VMEM((2, 2 * B, n), jnp.bfloat16),
            pltpu.VMEM((2, n, n), jnp.bfloat16), pltpu.VMEM((n, width), jnp.bfloat16), pltpu.SemaphoreType.DMA((n // (2 * B),))]


B=128
bf16=jnp.bfloat16; f32=jnp.float32

def dot_nt(a, b):
    return lax.dot_general(a, b, (((1,), (1,)), ((), ())), preferred_element_type=f32)

MESH = pl.DeviceIdType.MESH
HALF = 768


def lead_kernel(slab_ref, iscale_ref, noise_ref, zl_out, zr_ref, zc_ref, w_ref,
                xs, xr, xls, xlr, s16, zlb, zlo, X, V, R, wst, zt, wsem, own_sem, ssem, rsem, *, width, lead, half):
    p = lax.axis_index("row")
    qq = lax.axis_index("col")
    z = qq // 2
    c = qq % 2
    y = p // 4
    x = p % 4
    k16 = pl.multiple_of((p * 4 + z) * 16, 16)
    nh = 16 * half

    def dev(pp, zz, cc):
        return (pp, zz * 2 + cc)

    def rot(v, d):
        return (v + d + 4) % 4

    def plane(dy, dx):
        return rot(y, dy) * 4 + rot(x, dx)

    plane_offsets = [(dy, dx) for dy in range(4) for dx in range(4) if (dy, dx) != (0, 0)]
    col_offsets = [(dz, dc) for dz in range(4) for dc in range(2) if (dz, dc) != (0, 0)]

    barrier = pltpu.get_barrier_semaphore()
    for dy, dx in plane_offsets:
        pl.semaphore_signal(barrier, inc=1, device_id=dev(plane(dy, dx), z, c), device_id_type=MESH)
    for dz, dc in col_offsets:
        pl.semaphore_signal(barrier, inc=1, device_id=dev(p, rot(z, dz), (c + dc) % 2), device_id_type=MESH)

    def remote(src, dst, i, target):
        return pltpu.make_async_remote_copy(src_ref=src, dst_ref=dst, send_sem=ssem.at[i], recv_sem=rsem.at[i],
                                            device_id=target, device_id_type=MESH)

    def step_a(pp, d):
        yy, xx = pp // 4, pp % 4
        return (yy * 4 + rot(xx, d)) * (1 - c) + (rot(yy, d) * 4 + xx) * c

    def step_b(pp, d):
        yy, xx = pp // 4, pp % 4
        return (yy * 4 + rot(xx, d)) * c + (rot(yy, d) * 4 + xx) * (1 - c)

    def block(pp):
        return pl.ds(pl.multiple_of(pp * 64, 64), 64)

    base = {}
    at = 0
    for name, n in (("X", 2), ("L1", 3), ("L2", 15), ("LP", 15), ("LZ", 3), ("PF", 16), ("PZ", 4), ("CA", 7), ("RA", 15), ("A1", 2), ("A2", 2),
                    ("B1", 8), ("B2", 8), ("Z1", 2), ("Z2", 2), ("PR", 1)):
        base[name] = at
        at += n
    DS = (0, 1, -1, 2)

    def exchange_lead():
        return [remote(xls, xlr, base["X"], dev(p, z, 1 - c))]

    def exchange():
        return [remote(xs, xr, base["X"] + 1, dev(p, z, 1 - c))]

    def first0():
        r = zlb.at[0, p, z]
        return [remote(r, r, base["L1"] + d - 1, dev(p, rot(z, d), c)) for d in (1, 2, 3)]

    def second0():
        r = zlb.at[0, p]
        return [remote(r, r, base["L2"] + n, dev(plane(dy, dx), z, c)) for n, (dy, dx) in enumerate(plane_offsets)]

    def pass0(n):
        src = p if n == 15 else plane(-plane_offsets[n][0], -plane_offsets[n][1])
        r = zlb.at[0, src]
        return [remote(r, r, base["PF"] + n, dev(p, z, 1 - c))]

    def first1():
        r = zlb.at[1, p, z]
        return [remote(r, r, base["LP"] + n, dev(plane(dy, dx), z, c)) for n, (dy, dx) in enumerate(plane_offsets)]

    def second1():
        r = zlb.at[1, :, z]
        return [remote(r, r, base["LZ"] + d - 1, dev(p, rot(z, d), c)) for d in (1, 2, 3)]

    def pass1(d):
        r = zlb.at[1, :, rot(z, -d)]
        return [remote(r, r, base["PZ"] + d, dev(p, z, 1 - c))]

    def col_a2a():
        out = []
        for n, (dz, dc) in enumerate(col_offsets):
            zz, cc = rot(z, dz), (c + dc) % 2
            out.append(remote(s16.at[:, zz * 2 + cc], zc_ref.at[:, c, pl.ds(k16, 16), :], base["CA"] + n, dev(p, zz, cc)))
        return out

    def row_a2a():
        out = []
        for n, (dy, dx) in enumerate(plane_offsets):
            pp = plane(dy, dx)
            out.append(remote(s16.at[pp // 8, pp % 8], zr_ref.at[c, p, z], base["RA"] + n, dev(pp, z, c)))
        return out

    def own_copies():
        return [pltpu.make_async_copy(s16.at[:, qq], zc_ref.at[:, c, pl.ds(k16, 16), :], own_sem.at[0]),
                pltpu.make_async_copy(s16.at[p // 8, p % 8], zr_ref.at[c, p, z], own_sem.at[1])]

    def a1():
        r = zc_ref.at[:, :, block(p), :]
        return [remote(r, r, base["A1"], dev(step_a(p, 1), z, c)), remote(r, r, base["A1"] + 1, dev(step_a(p, -1), z, c))]

    def a2():
        f = zc_ref.at[0, :, block(step_a(p, -1)), :]
        g = zc_ref.at[1, :, block(step_a(p, 1)), :]
        return [remote(f, f, base["A2"], dev(step_a(p, 1), z, c)), remote(g, g, base["A2"] + 1, dev(step_a(p, -1), z, c))]

    def b1(n):
        r = zc_ref.at[:, :, block(step_a(p, DS[n])), :]
        return [remote(r, r, base["B1"] + 2 * n, dev(step_b(p, 1), z, c)),
                remote(r, r, base["B1"] + 2 * n + 1, dev(step_b(p, -1), z, c))]

    def b2(n):
        f = zc_ref.at[0, :, block(step_a(step_b(p, -1), DS[n])), :]
        g = zc_ref.at[1, :, block(step_a(step_b(p, 1), DS[n])), :]
        return [remote(f, f, base["B2"] + 2 * n, dev(step_b(p, 1), z, c)),
                remote(g, g, base["B2"] + 2 * n + 1, dev(step_b(p, -1), z, c))]

    def z1():
        r = zr_ref.at[c, :, z]
        return [remote(r, r, base["Z1"], dev(p, rot(z, 1), c)), remote(r, r, base["Z1"] + 1, dev(p, rot(z, -1), c))]

    def z2():
        f = zr_ref.at[c, 0:8, rot(z, -1)]
        g = zr_ref.at[c, 8:16, rot(z, 1)]
        return [remote(f, f, base["Z2"], dev(p, rot(z, 1), c)), remote(g, g, base["Z2"] + 1, dev(p, rot(z, -1), c))]

    def partner_rows():
        r = zr_ref.at[c]
        return [remote(r, r, base["PR"], dev(p, z, 1 - c))]

    def start(copies):
        for cp in copies:
            cp.start()

    def arrived(copies):
        for cp in copies:
            cp.wait_recv()

    number = p * 8 + qq
    lanes = lax.broadcasted_iota(jnp.int32, (8, B), 1)
    subs = lax.broadcasted_iota(jnp.int32, (8, B), 0)
    line = jnp.broadcast_to(iscale_ref[pl.ds(number // 16, 1), :], (8, B))
    scale = jnp.sum(jnp.where(lanes == subs + (number % 16) * 8, line, 0.0), axis=1, keepdims=True)

    def scaled(sl):
        return (slab_ref[:, sl].astype(f32) * scale).astype(bf16).astype(f32)

    def pair(own, other):
        first = own * (1 - c).astype(f32) + other * c.astype(f32)
        second = other * (1 - c).astype(f32) + own * c.astype(f32)
        return jnp.concatenate([first, second], axis=0).astype(bf16)

    xls[...] = scaled(slice(0, lead))
    pl.semaphore_wait(barrier, len(plane_offsets) + len(col_offsets))
    start(exchange_lead())
    CH = 2048
    for h in range(2):
        @pl.when(c == 1 - h)
        def _():
            for o in range(0, nh, CH):
                xs[:, o:o + CH] = scaled(slice(h * nh + o, h * nh + o + CH))
    start(exchange())
    arrived(exchange_lead())
    for j in range(lead // B // 2):
        for h in range(2):
            @pl.when(c == h)
            def _():
                o = (2 * j + h) * B
                zlb[h, p, z, :, j * B:(j + 1) * B] = pair(xls[:, o:o + B], xlr[:, o:o + B])

    @pl.when(c == 0)
    def _():
        start(first0())

    @pl.when(c == 1)
    def _():
        start(first1())
    arrived(exchange())
    for h in range(2):
        @pl.when(c == h)
        def _():
            for a in range(half // B):
                own = scaled(slice(h * nh + a * 2048, h * nh + (a + 1) * 2048))
                both = pair(own, xr[:, a * 2048:(a + 1) * 2048])
                for s in range(16):
                    s16[s // 8, s % 8, :, a * B:(a + 1) * B] = both[:, s * B:(s + 1) * B]

    @pl.when(c == 0)
    def _():
        arrived(first0())
        start(second0())
        start(pass0(15))
        for n, cp in enumerate(second0()):
            cp.wait_recv()
            start(pass0(n))

    @pl.when(c == 1)
    def _():
        arrived(first1())
        start(second1())
        start(pass1(0))
        for n, cp in enumerate(second1()):
            cp.wait_recv()
            start(pass1(n + 1))
    start(col_a2a())
    start(own_copies())
    start(row_a2a())

    @pl.when(c == 0)
    def _():
        for d in range(4):
            arrived(pass1(d))

    @pl.when(c == 1)
    def _():
        for n in range(16):
            arrived(pass0(n))

    for u in range(lead // B):
        zlo[:, u * B:(u + 1) * B] = zlb[u % 2, :, :, :, (u // 2) * B:(u // 2 + 1) * B].reshape(width, B)
    zl_copy = pltpu.make_async_copy(zlo, zl_out, own_sem.at[2])
    zl_copy.start()

    def poll(b):
        @pl.when(b == 0)
        def _():
            for cp in own_copies():
                cp.wait()
            arrived(col_a2a())
            start(a1())
            arrived(row_a2a())
            start(z1())

        @pl.when(b == 1)
        def _():
            start(b1(0))

        @pl.when(b == 2)
        def _():
            arrived(a1())
            start(a2())
            start(b1(1))
            start(b1(2))
            arrived(z1())
            start(z2())

        @pl.when(b == 3)
        def _():
            arrived(a2())
            start(b1(3))

        @pl.when(b == 4)
        def _():
            arrived(z2())
            start(partner_rows())
            arrived(b1(0))
            start(b2(0))

        @pl.when(b == 5)
        def _():
            for n in (1, 2):
                arrived(b1(n))
                start(b2(n))

        @pl.when(b == 6)
        def _():
            arrived(b1(3))
            start(b2(3))

    chol_body(zlo, noise_ref, w_ref, X, V, R, wst, zt, wsem, lead, width, poll)
    for n in range(4):
        arrived(b2(n))
    arrived(partner_rows())
    zl_copy.wait()
    chol_done(w_ref, wst, wsem, lead)
    sent = exchange_lead() + exchange() + col_a2a() + row_a2a() + a1() + a2() + z1() + z2() + partner_rows()
    for n in range(4):
        sent += b1(n) + b2(n)
    for cp in sent:
        cp.wait_send()

    @pl.when(c == 0)
    def _():
        last = first0() + second0()
        for n in range(16):
            last += pass0(n)
        for cp in last:
            cp.wait_send()

    @pl.when(c == 1)
    def _():
        last = first1() + second1()
        for d in range(4):
            last += pass1(d)
        for cp in last:
            cp.wait_send()


def lead_call(slab, scale, noise, lead, width):
    total = slab.shape[1]
    half = total // 32
    o = jax.ShapeDtypeStruct((2, lead, lead), bf16)
    vm = pl.BlockSpec(memory_space=pltpu.VMEM)
    hbm = pl.BlockSpec(memory_space=pltpu.HBM)
    nsem = 107
    return pl.pallas_call(
        functools.partial(lead_kernel, width=width, lead=lead, half=half),
        out_shape=(jax.ShapeDtypeStruct((width, lead), bf16), jax.ShapeDtypeStruct((2, 16, 4, 16, half), bf16),
                   jax.ShapeDtypeStruct((2, 2, width, half), bf16), o),
        in_specs=[vm, vm, vm],
        out_specs=[hbm] * 4,
        scratch_shapes=[pltpu.VMEM((8, 16 * half), f32), pltpu.VMEM((8, 16 * half), f32),
                        pltpu.VMEM((8, lead), f32), pltpu.VMEM((8, lead), f32),
                        pltpu.VMEM((2, 8, 16, half), bf16), pltpu.VMEM((2, 16, 4, 16, lead // 2), bf16),
                        pltpu.VMEM((width, lead), bf16)] + chol_scratch(lead, width) + [pltpu.SemaphoreType.DMA((3,)),
                        pltpu.SemaphoreType.DMA((nsem,)), pltpu.SemaphoreType.DMA((nsem,))],
        compiler_params=pltpu.CompilerParams(vmem_limit_bytes=60 * 2**20, collective_id=0, has_side_effects=True),
    )(slab, scale, noise)


def main_body(zl_hbm, zr_hbm, zc_hbm, w_hbm, nz_ref, out_ref, fac_ref,
              zl_ref, zr_ref, zc_ref, w_ref, zlt, zrt, kh, kl, lh, ll, gh, gl, dh, mus, g1, hr, hlc, stage, isem, sem,
              *, width, lead, nrow, ncol, RT=512, CT=768):
    half = zr_ref.shape[2]; rows = 2 * half
    p = lax.axis_index("row")
    q = lax.axis_index("col")
    cs = LOG2E / (2 * width)
    loads = [pltpu.make_async_copy(a, b, isem.at[n]) for n, (a, b) in enumerate(
        ((zl_hbm, zl_ref), (zr_hbm, zr_ref), (w_hbm, w_ref), (zc_hbm, zc_ref)))]
    for cp in loads:
        cp.start()
    loads[0].wait()
    for i in range(0, lead, 256):
        zlt[i:i+256, :] = zl_ref[:, i:i+256].T
    def colsq(ref, sl):
        x = ref[:, sl].astype(f32)
        return jnp.sum(x * x, axis=0, keepdims=True) * cs
    def lanecol(v):
        return jnp.broadcast_to(jnp.broadcast_to(v, (8, v.shape[1])).T[:, 0:1], (v.shape[1], B))
    for i in range(0, lead, 256):
        hlc[i:i+256, :] = lanecol(colsq(zl_ref, slice(i, i+256)))
    loads[1].wait()
    for i in range(0, rows, 256):
        part = zr_ref.at[i // half]
        o = i % half
        zrt[i:i+256, :] = part[:, o:o+256].T
        hr[i:i+256, :] = lanecol(colsq(part, slice(o, o+256)))
    def wide(x, n):
        return jnp.concatenate([x] * (n // B), axis=1)
    for j in range(0, lead, 256):
        hl = colsq(zl_ref, slice(j, j + 256))
        for i in range(0, rows, RT):
            t = dot(zrt[i:i+RT, :], zl_ref[:, j:j+256]) * (2 * cs) - wide(hr[i:i+RT, :], 256) - hl
            k = jnp.exp2(t)
            if i == 0:
                ri = lax.broadcasted_iota(jnp.int32, (B, 256), 0) + p * B
                ci = lax.broadcasted_iota(jnp.int32, (B, 256), 1) + j
                nug = jnp.where(ri == ci, jnp.broadcast_to(jnp.concatenate([nz_ref[j//B:j//B+1, :], nz_ref[j//B+1:j//B+2, :]], axis=1), (B, 256)), 0.0)
                k = jnp.concatenate([k[:B] + nug, k[B:]], axis=0)
            h, l = split(k)
            kh[i:i+RT, j:j+256] = h
            kl[i:i+RT, j:j+256] = l
    loads[2].wait()
    for j in range(0, lead, 256):
        e = j + 256
        for i in range(0, rows, RT):
            rs = slice(i, i + RT)
            x = dot_nt(kh[rs, :e], w_ref[0, j:e, :e]) + dot_nt(kh[rs, :e], w_ref[1, j:e, :e]) + dot_nt(kl[rs, :e], w_ref[0, j:e, :e])
            h, l = split(x)
            lh[rs, j:e] = h
            ll[rs, j:e] = l
            for hb in range(2):
                @pl.when(q == j // B + hb)
                def _():
                    fac_ref[rs, :] = x[:, hb * B:(hb + 1) * B]
    @pl.when(p * B < lead)
    def _():
        ri = lax.broadcasted_iota(jnp.int32, (B, B), 0) + p * B
        ci = lax.broadcasted_iota(jnp.int32, (B, B), 1) + q * B
        fac_ref[:B, :] = jnp.where(ri >= ci, fac_ref[:B, :], 0.0)
    gsq = [None] * (lead // 256)
    for i in range(0, rows, RT):
        rs = slice(i, i + RT)
        tot = None
        for j in range(0, lead, 256):
            x = dot(lh[rs, j:], w_ref[0, j:, j:j+256]) + dot(lh[rs, j:], w_ref[1, j:, j:j+256]) + dot(ll[rs, j:], w_ref[0, j:, j:j+256])
            h, l = split(x)
            gh[rs, j:j+256] = h
            gl[rs, j:j+256] = l
            sm = jnp.sum(x, axis=1, keepdims=True)
            tot = sm if tot is None else tot + sm
            xx = x * x
            if i == 0:
                live = jnp.where(p * B < lead, 0.0, 1.0)
                xx = jnp.concatenate([xx[:B] * live, xx[B:]], axis=0)
            sq = jnp.sum(xx, axis=0, keepdims=True)
            n = j // 256
            gsq[n] = sq if gsq[n] is None else gsq[n] + sq
        g1[rs, :] = jnp.broadcast_to(tot, (RT, B))
    nzs = nz_ref[...]
    limit = jnp.sum(nzs * nzs) * (0.0018 ** 2 * rows * CT / float(nzs.shape[0] * B) ** 2)
    gs = jnp.broadcast_to(jnp.concatenate(gsq, axis=1), (8, lead))
    loads[3].wait()
    nch = 4 * half // CT
    bc = CT // B
    per = half // CT
    def col_block(c, u):
        g = c // per
        return 2 * ((g % 2) * (half // B) + (c % per) * bc + u) + g // 2
    def copies(c, slot, i):
        return [pltpu.make_async_copy(stage.at[slot, pl.ds(i, RT), pl.ds(u * B, B)],
                                      out_ref.at[pl.ds(i, RT), col_block(c, u), 0, :], sem.at[slot, i // RT, u]) for u in range(bc)]
    LT = 256
    def finish(c, slot, i):
        for u in range(bc):
            gb = col_block(c, u) * ncol + q
            a = gb // nrow
            @pl.when((gb % nrow == p) & (a * B >= i) & (a * B < i + RT))
            def _():
                r0 = pl.multiple_of(a * B, B)
                ri = lax.broadcasted_iota(jnp.int32, (B, B), 0)
                ci = lax.broadcasted_iota(jnp.int32, (B, B), 1)
                nzv = nz_ref[pl.ds(gb, 1), :]
                at = (slot, pl.ds(r0, B), slice(u*B, (u+1)*B))
                stage[at] = stage[at] + jnp.where(ri == ci, jnp.broadcast_to(nzv, (B, B)), 0.0)
            @pl.when(gb * B < lead)
            def _():
                stage[slot, i:i+RT, u*B:(u+1)*B] = jnp.zeros((RT, B), f32)
        if i == 0:
            @pl.when(p * B < lead)
            def _():
                stage[slot, :B, :] = jnp.zeros((B, CT), f32)
        for cp in copies(c, slot, i): cp.start()

    def chunk(c, _):
        slot = lax.rem(c, 2)
        c0 = pl.multiple_of((c % per) * CT, CT)
        zc = zc_ref[c // per, :, pl.ds(c0, CT)]
        x = zc.astype(f32)
        hc = jnp.sum(x * x, axis=0, keepdims=True) * cs
        mu = None
        gd = None
        for i in range(0, lead, LT):
            kc = jnp.exp2(dot(zlt[i:i+LT, :], zc) * (2 * cs) - wide(hlc[i:i+LT, :], CT) - hc)
            if mu is None:
                mu = jnp.mean(kc, axis=0, keepdims=True)
                mus[...] = jnp.broadcast_to(mu, (8, CT))
            dd = kc - mu
            dh[i:i+LT, :] = dd.astype(bf16)
            d2 = dd * dd
            ds = None
            for u in range(bc):
                live = jnp.where((col_block(c, u) * ncol + q) * B < lead, 0.0, 1.0)
                du = d2[:, u*B:(u+1)*B] * live
                ds = du if ds is None else ds + du
            part = dot(gs[:, i:i+LT], ds)
            gd = part if gd is None else gd + part
        err = jnp.sum(gd) * (1.0 / 8) * (2.0 * 2.0 ** -19)
        good = err <= limit
        @pl.when(c >= 2)
        def _():
            for i in range(0, rows, RT):
                for cp in copies(c, slot, i): cp.wait()
        @pl.when(good)
        def _():
            for i in range(0, rows, RT):
                rs = slice(i, i + RT)
                k = jnp.exp2(dot(zrt[rs, :], zc) * (2 * cs) - wide(hr[rs, :], CT) - hc)
                stage[slot, rs, :] = k - dot(gh[rs, :], dh[...]) - wide(g1[rs, :], CT) * mu
                finish(c, slot, i)
        @pl.when(jnp.logical_not(good))
        def _():
            def rowtile(n, _):
                rs = pl.ds(pl.multiple_of(n * 256, 256), 256)
                k = jnp.exp2(dot(zrt[rs, :], zc) * (2 * cs) - wide(hr[rs, :], CT) - hc)
                stage[slot, rs, :] = k - wide(g1[rs, :], CT) * mu
                return 0
            lax.fori_loop(0, rows // 256, rowtile, 0)
            def leadtile(m, _):
                ls = pl.ds(pl.multiple_of(m * LT, LT), LT)
                dd = jnp.exp2(dot(zlt[ls, :], zc) * (2 * cs) - wide(hlc[ls, :], CT) - hc) - mus[0:1, :]
                h, l = split(dd)
                def rt(n, _):
                    rs = pl.ds(pl.multiple_of(n * 256, 256), 256)
                    stage[slot, rs, :] = stage[slot, rs, :] - (dot(gh[rs, ls], h) + dot(gh[rs, ls], l) + dot(gl[rs, ls], h))
                    return 0
                lax.fori_loop(0, rows // 256, rt, 0)
                return 0
            lax.fori_loop(0, lead // LT, leadtile, 0)
            for i in range(0, rows, RT):
                finish(c, slot, i)
        return 0
    lax.fori_loop(0, nch, chunk, 0)
    for c in (nch - 2, nch - 1):
        for i in range(0, rows, RT):
            for cp in copies(c, c % 2, i): cp.wait()

def main_call(zl, zr, zc, w, nz, nrow=16, ncol=8):
    width, lead = zl.shape; half = zr.shape[2]; rows = 2 * half; cols = 4 * half
    V = pl.BlockSpec(memory_space=pltpu.VMEM)
    H = pl.BlockSpec(memory_space=pltpu.HBM)
    CT = 768
    return pl.pallas_call(functools.partial(main_body, width=width, lead=lead, nrow=nrow, ncol=ncol, CT=CT),
        out_shape=(jax.ShapeDtypeStruct((rows, cols // B, 1, B), f32), jax.ShapeDtypeStruct((rows, B), f32)),
        in_specs=[H, H, H, H, V],
        out_specs=(H, V),
        scratch_shapes=[pltpu.VMEM(zl.shape, bf16), pltpu.VMEM(zr.shape, bf16), pltpu.VMEM(zc.shape, bf16), pltpu.VMEM(w.shape, bf16),
          pltpu.VMEM((lead, width), bf16), pltpu.VMEM((rows, width), bf16)] +
          [pltpu.VMEM((rows, lead), bf16)] * 6 + [pltpu.VMEM((lead, CT), bf16), pltpu.VMEM((8, CT), f32)] +
          [pltpu.VMEM((rows, B), f32)] * 2 + [pltpu.VMEM((lead, B), f32),
          pltpu.VMEM((2, rows, CT), f32), pltpu.SemaphoreType.DMA((4,)), pltpu.SemaphoreType.DMA((2, 3, CT // B))],
        compiler_params=pltpu.CompilerParams(vmem_limit_bytes=61*2**20),
    )(zl, zr, zc, w, nz)


def body(embeddings, inv_scale, noise):
    nrow = lax.axis_size("row")
    ncol = lax.axis_size("col")
    total, fdev = embeddings.shape
    width = inv_scale.shape[0]
    crow = total // (TILE * nrow)
    ccol = total // (TILE * ncol)
    lead = PANELS * PB
    nz = noise.reshape(total // TILE, TILE)
    zl, zr, zc, w = lead_call(embeddings.T, inv_scale.reshape(width // TILE, TILE), nz, lead, width)
    half = zr.shape[-1]
    schur, factor = main_call(zl, zr.reshape(2, width, half), zc.reshape(4, width, half), w, nz,
                              nrow=nrow, ncol=ncol)
    return (
        factor.reshape(crow, 1, TILE, TILE),
        schur.reshape(crow, 1, TILE, ccol, 1, TILE),
    )


def solution(mesh):
    placed = (P(None, ("row", "col")), P(), P())
    return jax.shard_map(
        body,
        mesh=mesh,
        in_specs=placed,
        out_specs=(P(None, "row", None, "col"), P(None, "row", None, None, "col", None)),
        check_vma=False,
    )
```

```python
import functools
import math

import jax
import jax.numpy as jnp
from jax import lax
from jax.experimental import pallas as pl
from jax.experimental.pallas import tpu as pltpu
from jax.sharding import PartitionSpec as P

TILE = 128
PB = 512
PANELS = 2
B=128
def factor_block(load, store, look=2):
    lane = lax.broadcasted_iota(jnp.int32, (8, B), 1)
    sub = lax.broadcasted_iota(jnp.int32, (8, B), 0)
    G = B // 8
    X = [load(g) for g in range(G)]

    def across(v, j):
        return jnp.broadcast_to(v[:, j:j + 1], (8, B))

    def down(v, i):
        return jnp.broadcast_to(v[i:i + 1, :], (8, B))

    def rcp(d):
        r0 = pl.reciprocal(d, approx=True)
        return r0 * (2.0 - d * r0)

    for g in range(G):
        P = X[g]
        base = 8 * g
        c = [across(P, base + j) for j in range(8)]
        s = [[down(c[j], i) if j <= i else None for j in range(8)] for i in range(8)]
        ingroup = (lane >= base) & (lane < base + 8)
        Pp = jnp.where(ingroup, jnp.where(lane - base == sub, 1.0, 0.0), P)
        f = [down(Pp, k) for k in range(8)]
        near = g + 1 < G
        if near:
            nk = [across(X[g + 1], base + k) for k in range(8)]
            acc = jnp.where(ingroup, 0.0, X[g + 1])
        m = [[None] * 8 for _ in range(8)]
        h = [None] * 8
        out = [None] * 8
        for k in range(0, 8, 2):
            a, b, d = s[k][k], s[k + 1][k], s[k + 1][k + 1]
            det = a * d - b * b
            rd = rcp(det)
            for i in range(k + 2, 8):
                u0 = d * s[i][k] - b * s[i][k + 1]
                u1 = a * s[i][k + 1] - b * s[i][k]
                m[i][k] = u0 * rd
                m[i][k + 1] = u1 * rd
                for j in range(k + 2, i + 1):
                    s[i][j] = s[i][j] - (u0 * s[j][k] + u1 * s[j][k + 1]) * rd
            for i in range(k + 2, 8):
                f[i] = f[i] - (m[i][k] * f[k] + m[i][k + 1] * f[k + 1])
                if near:
                    nk[i] = nk[i] - (m[i][k] * nk[k] + m[i][k + 1] * nk[k + 1])
            h[k] = (d * f[k] - b * f[k + 1]) * rd
            h[k + 1] = (a * f[k + 1] - b * f[k]) * rd
            if near:
                acc = acc - (nk[k] * h[k] + nk[k + 1] * h[k + 1])
            ra = lax.rsqrt(a)
            ra2 = ra * ra
            out[k] = f[k] * ra
            out[k + 1] = (f[k + 1] - b * ra2 * f[k]) * lax.rsqrt(det * ra2)
        if near:
            X[g + 1] = acc
        fo = out[0]
        for k in range(1, 8):
            fo = jnp.where(sub == k, out[k], fo)
        store(g, fo)
        if g + 2 >= G:
            continue
        w = list(h)
        for k in range(4, -1, -2):
            for i in range(k + 2, 8):
                w[k] = w[k] - m[i][k] * w[i]
                w[k + 1] = w[k + 1] - m[i][k + 1] * w[i]
        for i in range(g + 2, min(g + 1 + look, G)):
            acc = jnp.where(ingroup, 0.0, X[i])
            for k in range(8):
                acc = acc - across(X[i], base + k) * w[k]
            X[i] = acc
        first = g + 1 + look
        if first >= G:
            continue
        w8 = w[0]
        for k in range(1, 8):
            w8 = jnp.where(sub == k, w[k], w8)
        parts = []
        if base:
            parts.append(jnp.zeros((base, B), jnp.float32))
        parts.append(w8)
        if base + 8 < B:
            parts.append(jnp.zeros((B - base - 8, B), jnp.float32))
        rh, rl = split(jnp.concatenate(parts, axis=0))
        rest = jnp.concatenate(X[first:], axis=0)
        inr = (lax.broadcasted_iota(jnp.int32, rest.shape, 1) >= base) & (lax.broadcasted_iota(jnp.int32, rest.shape, 1) < base + 8)
        lh, ll = split(jnp.where(inr, rest, 0.0))
        new = jnp.where(inr, 0.0, rest) - (dot(lh, rh) + dot(lh, rl) + dot(ll, rh))
        for i in range(first, G):
            X[i] = new[8 * (i - first):8 * (i - first) + 8]

def split(x):
    hi = x.astype(jnp.bfloat16)
    return hi, (x - hi.astype(jnp.float32)).astype(jnp.bfloat16)

def dot(a, b):
    return jnp.dot(a, b, preferred_element_type=jnp.float32)

def dot3(a, b):
    ah, al = a; bh, bl = b
    return dot(ah, bh) + dot(ah, bl) + dot(al, bh)

LOG2E = math.log2(math.e)

def chol_body(zl_ref, noise_ref, w_hbm, X, V, R, wst, zt, wsem, n, width, poll=None):
    D = 2 * B
    steps = n // D
    zf = zl_ref[...].astype(jnp.float32)
    hc = jnp.sum(zf * zf, axis=0, keepdims=True) * (LOG2E / (2 * width))
    hcol = jnp.broadcast_to(hc, (8, n)).T[:, 0:1]
    nzl = jnp.concatenate([noise_ref[i:i + 1, :] for i in range(n // B)], axis=1)
    for i in range(steps):
        lo = i * D
        rows = slice(lo, lo + D)
        zt[rows, :] = zl_ref[:, rows].T
        t = dot(zt[rows, :], zl_ref[:, lo:]) * (LOG2E / width) - hcol[rows, :] - hc[:, lo:]
        k = jnp.exp2(t)
        ri = lax.broadcasted_iota(jnp.int32, (D, n - lo), 0)
        ci = lax.broadcasted_iota(jnp.int32, (D, n - lo), 1)
        X[rows, lo:] = k + jnp.where(ri == ci, jnp.broadcast_to(nzl[:, lo:], (D, n - lo)), 0.0)
    tri = lax.broadcasted_iota(jnp.int32, (B, B), 0) >= lax.broadcasted_iota(jnp.int32, (B, B), 1)
    eye = jnp.where(lax.broadcasted_iota(jnp.int32, (B, B), 0) == lax.broadcasted_iota(jnp.int32, (B, B), 1), 1.0, 0.0)

    def eliminate(r0):
        factor_block(lambda g: X[pl.ds(r0 + 8 * g, 8), pl.ds(r0, B)], lambda g, v: V.__setitem__((pl.ds(8 * g, 8), slice(None)), v))
        v = jnp.where(tri, V[...], 0.0)
        X[pl.ds(r0, B), pl.ds(r0, B)] = eye
        X[pl.ds(r0, B), :] = dot3(split(v), split(X[pl.ds(r0, B), :]))

    def step(t, _):
        r0 = pl.multiple_of(t * D, D)
        r1 = pl.multiple_of(t * D + B, B)
        if poll is not None:
            poll(2 * t)
        eliminate(r0)
        T = X[pl.ds(r0, B), pl.ds(r1, B)].T
        X[pl.ds(r1, B), pl.ds(r0, B)] = jnp.zeros((B, B), jnp.float32)
        X[pl.ds(r1, B), :] = X[pl.ds(r1, B), :] - dot3(split(T), split(X[pl.ds(r0, B), :]))
        if poll is not None:
            poll(2 * t + 1)
        eliminate(r1)
        both = X[pl.ds(r0, D), :]
        ri = lax.broadcasted_iota(jnp.int32, (D, n), 0) + r0
        ci = lax.broadcasted_iota(jnp.int32, (D, n), 1)
        h, l = split(jnp.where(ri >= ci, both, 0.0))
        wst[0, pl.ds(r0, D), :] = h
        wst[1, pl.ds(r0, D), :] = l
        pltpu.make_async_copy(wst.at[:, pl.ds(r0, D), :], w_hbm.at[:, pl.ds(r0, D), :], wsem.at[t]).start()
        h, l = split(both)
        R[0] = h
        R[1] = l
        R[:, 0:B, pl.ds(r1, B)] = jnp.zeros((2, B, B), jnp.bfloat16)

        def upd(i, _):
            i0 = pl.multiple_of(i * D, D)
            T = X[pl.ds(r0, D), pl.ds(i0, D)].T
            X[pl.ds(i0, D), pl.ds(r0, D)] = jnp.zeros((D, D), jnp.float32)
            X[pl.ds(i0, D), :] = X[pl.ds(i0, D), :] - dot3(split(T), (R[0], R[1]))
            return 0
        lax.fori_loop(t + 1, steps, upd, 0)
        return 0
    lax.fori_loop(0, steps, step, 0)

def chol_done(w_hbm, wst, wsem, n):
    D = 2 * B
    for t in range(n // D):
        pltpu.make_async_copy(wst.at[:, pl.ds(t * D, D), :], w_hbm.at[:, pl.ds(t * D, D), :], wsem.at[t]).wait()

def chol_scratch(n, width):
    return [pltpu.VMEM((n, n), jnp.float32), pltpu.VMEM((B, B), jnp.float32), pltpu.VMEM((2, 2 * B, n), jnp.bfloat16),
            pltpu.VMEM((2, n, n), jnp.bfloat16), pltpu.VMEM((n, width), jnp.bfloat16), pltpu.SemaphoreType.DMA((n // (2 * B),))]


B=128
bf16=jnp.bfloat16; f32=jnp.float32

def dot_nt(a, b):
    return lax.dot_general(a, b, (((1,), (1,)), ((), ())), preferred_element_type=f32)

MESH = pl.DeviceIdType.MESH
HALF = 768


def lead_kernel(slab_ref, iscale_ref, noise_ref, zl_out, zr_ref, zc_ref, w_ref,
                xs, xr, xls, xlr, s16, zlb, zlo, X, V, R, wst, zt, wsem, own_sem, ssem, rsem, *, width, lead, half):
    p = lax.axis_index("row")
    qq = lax.axis_index("col")
    z = qq // 2
    c = qq % 2
    y = p // 4
    x = p % 4
    k16 = pl.multiple_of((p * 4 + z) * 16, 16)
    nh = 16 * half

    def dev(pp, zz, cc):
        return (pp, zz * 2 + cc)

    def rot(v, d):
        return (v + d + 4) % 4

    def plane(dy, dx):
        return rot(y, dy) * 4 + rot(x, dx)

    plane_offsets = [(dy, dx) for dy in range(4) for dx in range(4) if (dy, dx) != (0, 0)]
    col_offsets = [(dz, dc) for dz in range(4) for dc in range(2) if (dz, dc) != (0, 0)]

    barrier = pltpu.get_barrier_semaphore()
    for dy, dx in plane_offsets:
        pl.semaphore_signal(barrier, inc=1, device_id=dev(plane(dy, dx), z, c), device_id_type=MESH)
    for dz, dc in col_offsets:
        pl.semaphore_signal(barrier, inc=1, device_id=dev(p, rot(z, dz), (c + dc) % 2), device_id_type=MESH)

    def remote(src, dst, i, target):
        return pltpu.make_async_remote_copy(src_ref=src, dst_ref=dst, send_sem=ssem.at[i], recv_sem=rsem.at[i],
                                            device_id=target, device_id_type=MESH)

    def step_a(pp, d):
        yy, xx = pp // 4, pp % 4
        return (yy * 4 + rot(xx, d)) * (1 - c) + (rot(yy, d) * 4 + xx) * c

    def step_b(pp, d):
        yy, xx = pp // 4, pp % 4
        return (yy * 4 + rot(xx, d)) * c + (rot(yy, d) * 4 + xx) * (1 - c)

    def block(pp):
        return pl.ds(pl.multiple_of(pp * 64, 64), 64)

    base = {}
    at = 0
    for name, n in (("X", 2), ("L1", 3), ("L2", 15), ("LP", 15), ("LZ", 3), ("PF", 16), ("PZ", 4), ("CA", 7), ("RA", 15), ("A1", 2), ("A2", 2),
                    ("B1", 8), ("B2", 8), ("Z1", 2), ("Z2", 2), ("PR", 1)):
        base[name] = at
        at += n
    DS = (0, 1, -1, 2)

    def exchange_lead():
        return [remote(xls, xlr, base["X"], dev(p, z, 1 - c))]

    def exchange():
        return [remote(xs, xr, base["X"] + 1, dev(p, z, 1 - c))]

    def first0():
        r = zlb.at[0, p, z]
        return [remote(r, r, base["L1"] + d - 1, dev(p, rot(z, d), c)) for d in (1, 2, 3)]

    def second0():
        r = zlb.at[0, p]
        return [remote(r, r, base["L2"] + n, dev(plane(dy, dx), z, c)) for n, (dy, dx) in enumerate(plane_offsets)]

    def pass0(n):
        src = p if n == 15 else plane(-plane_offsets[n][0], -plane_offsets[n][1])
        r = zlb.at[0, src]
        return [remote(r, r, base["PF"] + n, dev(p, z, 1 - c))]

    def first1():
        r = zlb.at[1, p, z]
        return [remote(r, r, base["LP"] + n, dev(plane(dy, dx), z, c)) for n, (dy, dx) in enumerate(plane_offsets)]

    def second1():
        r = zlb.at[1, :, z]
        return [remote(r, r, base["LZ"] + d - 1, dev(p, rot(z, d), c)) for d in (1, 2, 3)]

    def pass1(d):
        r = zlb.at[1, :, rot(z, -d)]
        return [remote(r, r, base["PZ"] + d, dev(p, z, 1 - c))]

    def col_a2a():
        out = []
        for n, (dz, dc) in enumerate(col_offsets):
            zz, cc = rot(z, dz), (c + dc) % 2
            out.append(remote(s16.at[:, zz * 2 + cc], zc_ref.at[:, c, pl.ds(k16, 16), :], base["CA"] + n, dev(p, zz, cc)))
        return out

    def row_a2a():
        out = []
        for n, (dy, dx) in enumerate(plane_offsets):
            pp = plane(dy, dx)
            out.append(remote(s16.at[pp // 8, pp % 8], zr_ref.at[c, p, z], base["RA"] + n, dev(pp, z, c)))
        return out

    def own_copies():
        return [pltpu.make_async_copy(s16.at[:, qq], zc_ref.at[:, c, pl.ds(k16, 16), :], own_sem.at[0]),
                pltpu.make_async_copy(s16.at[p // 8, p % 8], zr_ref.at[c, p, z], own_sem.at[1])]

    def a1():
        r = zc_ref.at[:, :, block(p), :]
        return [remote(r, r, base["A1"], dev(step_a(p, 1), z, c)), remote(r, r, base["A1"] + 1, dev(step_a(p, -1), z, c))]

    def a2():
        f = zc_ref.at[0, :, block(step_a(p, -1)), :]
        g = zc_ref.at[1, :, block(step_a(p, 1)), :]
        return [remote(f, f, base["A2"], dev(step_a(p, 1), z, c)), remote(g, g, base["A2"] + 1, dev(step_a(p, -1), z, c))]

    def b1(n):
        r = zc_ref.at[:, :, block(step_a(p, DS[n])), :]
        return [remote(r, r, base["B1"] + 2 * n, dev(step_b(p, 1), z, c)),
                remote(r, r, base["B1"] + 2 * n + 1, dev(step_b(p, -1), z, c))]

    def b2(n):
        f = zc_ref.at[0, :, block(step_a(step_b(p, -1), DS[n])), :]
        g = zc_ref.at[1, :, block(step_a(step_b(p, 1), DS[n])), :]
        return [remote(f, f, base["B2"] + 2 * n, dev(step_b(p, 1), z, c)),
                remote(g, g, base["B2"] + 2 * n + 1, dev(step_b(p, -1), z, c))]

    def z1():
        r = zr_ref.at[c, :, z]
        return [remote(r, r, base["Z1"], dev(p, rot(z, 1), c)), remote(r, r, base["Z1"] + 1, dev(p, rot(z, -1), c))]

    def z2():
        f = zr_ref.at[c, 0:8, rot(z, -1)]
        g = zr_ref.at[c, 8:16, rot(z, 1)]
        return [remote(f, f, base["Z2"], dev(p, rot(z, 1), c)), remote(g, g, base["Z2"] + 1, dev(p, rot(z, -1), c))]

    def partner_rows():
        r = zr_ref.at[c]
        return [remote(r, r, base["PR"], dev(p, z, 1 - c))]

    def start(copies):
        for cp in copies:
            cp.start()

    def arrived(copies):
        for cp in copies:
            cp.wait_recv()

    number = p * 8 + qq
    lanes = lax.broadcasted_iota(jnp.int32, (8, B), 1)
    subs = lax.broadcasted_iota(jnp.int32, (8, B), 0)
    line = jnp.broadcast_to(iscale_ref[pl.ds(number // 16, 1), :], (8, B))
    scale = jnp.sum(jnp.where(lanes == subs + (number % 16) * 8, line, 0.0), axis=1, keepdims=True)

    def scaled(sl):
        return (slab_ref[:, sl].astype(f32) * scale).astype(bf16).astype(f32)

    def pair(own, other):
        first = own * (1 - c).astype(f32) + other * c.astype(f32)
        second = other * (1 - c).astype(f32) + own * c.astype(f32)
        return jnp.concatenate([first, second], axis=0).astype(bf16)

    xls[...] = scaled(slice(0, lead))
    pl.semaphore_wait(barrier, len(plane_offsets) + len(col_offsets))
    start(exchange_lead())
    CH = 2048
    for h in range(2):
        @pl.when(c == 1 - h)
        def _():
            for o in range(0, nh, CH):
                xs[:, o:o + CH] = scaled(slice(h * nh + o, h * nh + o + CH))
    start(exchange())
    arrived(exchange_lead())
    for j in range(lead // B // 2):
        for h in range(2):
            @pl.when(c == h)
            def _():
                o = (2 * j + h) * B
                zlb[h, p, z, :, j * B:(j + 1) * B] = pair(xls[:, o:o + B], xlr[:, o:o + B])

    @pl.when(c == 0)
    def _():
        start(first0())

    @pl.when(c == 1)
    def _():
        start(first1())
    arrived(exchange())
    for h in range(2):
        @pl.when(c == h)
        def _():
            for a in range(half // B):
                own = scaled(slice(h * nh + a * 2048, h * nh + (a + 1) * 2048))
                both = pair(own, xr[:, a * 2048:(a + 1) * 2048])
                for s in range(16):
                    s16[s // 8, s % 8, :, a * B:(a + 1) * B] = both[:, s * B:(s + 1) * B]

    @pl.when(c == 0)
    def _():
        arrived(first0())
        start(second0())
        start(pass0(15))
        for n, cp in enumerate(second0()):
            cp.wait_recv()
            start(pass0(n))

    @pl.when(c == 1)
    def _():
        arrived(first1())
        start(second1())
        start(pass1(0))
        for n, cp in enumerate(second1()):
            cp.wait_recv()
            start(pass1(n + 1))
    start(col_a2a())
    start(own_copies())
    start(row_a2a())

    @pl.when(c == 0)
    def _():
        for d in range(4):
            arrived(pass1(d))

    @pl.when(c == 1)
    def _():
        for n in range(16):
            arrived(pass0(n))

    for u in range(lead // B):
        zlo[:, u * B:(u + 1) * B] = zlb[u % 2, :, :, :, (u // 2) * B:(u // 2 + 1) * B].reshape(width, B)
    zl_copy = pltpu.make_async_copy(zlo, zl_out, own_sem.at[2])
    zl_copy.start()

    def poll(b):
        @pl.when(b == 0)
        def _():
            for cp in own_copies():
                cp.wait()
            arrived(col_a2a())
            start(a1())
            start(b1(0))
            arrived(row_a2a())
            start(z1())

        @pl.when(b == 2)
        def _():
            arrived(a1())
            start(a2())
            start(b1(1))
            start(b1(2))
            arrived(z1())
            start(z2())

        @pl.when(b == 3)
        def _():
            arrived(a2())
            start(b1(3))
            arrived(b1(0))
            start(b2(0))

        @pl.when(b == 4)
        def _():
            arrived(z2())
            start(partner_rows())

        @pl.when(b == 5)
        def _():
            for n in (1, 2):
                arrived(b1(n))
                start(b2(n))

        @pl.when(b == 6)
        def _():
            arrived(b1(3))
            start(b2(3))

    chol_body(zlo, noise_ref, w_ref, X, V, R, wst, zt, wsem, lead, width, poll)
    for n in range(4):
        arrived(b2(n))
    arrived(partner_rows())
    zl_copy.wait()
    chol_done(w_ref, wst, wsem, lead)
    sent = exchange_lead() + exchange() + col_a2a() + row_a2a() + a1() + a2() + z1() + z2() + partner_rows()
    for n in range(4):
        sent += b1(n) + b2(n)
    for cp in sent:
        cp.wait_send()

    @pl.when(c == 0)
    def _():
        last = first0() + second0()
        for n in range(16):
            last += pass0(n)
        for cp in last:
            cp.wait_send()

    @pl.when(c == 1)
    def _():
        last = first1() + second1()
        for d in range(4):
            last += pass1(d)
        for cp in last:
            cp.wait_send()


def lead_call(slab, scale, noise, lead, width):
    total = slab.shape[1]
    half = total // 32
    o = jax.ShapeDtypeStruct((2, lead, lead), bf16)
    vm = pl.BlockSpec(memory_space=pltpu.VMEM)
    hbm = pl.BlockSpec(memory_space=pltpu.HBM)
    nsem = 107
    return pl.pallas_call(
        functools.partial(lead_kernel, width=width, lead=lead, half=half),
        out_shape=(jax.ShapeDtypeStruct((width, lead), bf16), jax.ShapeDtypeStruct((2, 16, 4, 16, half), bf16),
                   jax.ShapeDtypeStruct((2, 2, width, half), bf16), o),
        in_specs=[vm, vm, vm],
        out_specs=[hbm] * 4,
        scratch_shapes=[pltpu.VMEM((8, 16 * half), f32), pltpu.VMEM((8, 16 * half), f32),
                        pltpu.VMEM((8, lead), f32), pltpu.VMEM((8, lead), f32),
                        pltpu.VMEM((2, 8, 16, half), bf16), pltpu.VMEM((2, 16, 4, 16, lead // 2), bf16),
                        pltpu.VMEM((width, lead), bf16)] + chol_scratch(lead, width) + [pltpu.SemaphoreType.DMA((3,)),
                        pltpu.SemaphoreType.DMA((nsem,)), pltpu.SemaphoreType.DMA((nsem,))],
        compiler_params=pltpu.CompilerParams(vmem_limit_bytes=60 * 2**20, collective_id=0, has_side_effects=True),
    )(slab, scale, noise)


def main_body(zl_hbm, zr_hbm, zc_hbm, w_hbm, nz_ref, out_ref, fac_ref,
              zl_ref, zr_ref, zc_ref, w_ref, zlt, zrt, kh, kl, lh, ll, gh, gl, dh, mus, g1, hr, hlc, stage, isem, sem,
              *, width, lead, nrow, ncol, RT=512, CT=768):
    half = zr_ref.shape[2]; rows = 2 * half
    p = lax.axis_index("row")
    q = lax.axis_index("col")
    cs = LOG2E / (2 * width)
    loads = [pltpu.make_async_copy(a, b, isem.at[n]) for n, (a, b) in enumerate(
        ((zl_hbm, zl_ref), (zr_hbm, zr_ref), (w_hbm, w_ref), (zc_hbm, zc_ref)))]
    for cp in loads:
        cp.start()
    loads[0].wait()
    for i in range(0, lead, 256):
        zlt[i:i+256, :] = zl_ref[:, i:i+256].T
    def colsq(ref, sl):
        x = ref[:, sl].astype(f32)
        return jnp.sum(x * x, axis=0, keepdims=True) * cs
    def lanecol(v):
        return jnp.broadcast_to(jnp.broadcast_to(v, (8, v.shape[1])).T[:, 0:1], (v.shape[1], B))
    for i in range(0, lead, 256):
        hlc[i:i+256, :] = lanecol(colsq(zl_ref, slice(i, i+256)))
    loads[1].wait()
    for i in range(0, rows, 256):
        part = zr_ref.at[i // half]
        o = i % half
        zrt[i:i+256, :] = part[:, o:o+256].T
        hr[i:i+256, :] = lanecol(colsq(part, slice(o, o+256)))
    def wide(x, n):
        return jnp.concatenate([x] * (n // B), axis=1)
    for j in range(0, lead, 256):
        hl = colsq(zl_ref, slice(j, j + 256))
        for i in range(0, rows, RT):
            t = dot(zrt[i:i+RT, :], zl_ref[:, j:j+256]) * (2 * cs) - wide(hr[i:i+RT, :], 256) - hl
            k = jnp.exp2(t)
            if i == 0:
                ri = lax.broadcasted_iota(jnp.int32, (B, 256), 0) + p * B
                ci = lax.broadcasted_iota(jnp.int32, (B, 256), 1) + j
                nug = jnp.where(ri == ci, jnp.broadcast_to(jnp.concatenate([nz_ref[j//B:j//B+1, :], nz_ref[j//B+1:j//B+2, :]], axis=1), (B, 256)), 0.0)
                k = jnp.concatenate([k[:B] + nug, k[B:]], axis=0)
            h, l = split(k)
            kh[i:i+RT, j:j+256] = h
            kl[i:i+RT, j:j+256] = l
    loads[2].wait()
    for j in range(0, lead, 256):
        e = j + 256
        for i in range(0, rows, RT):
            rs = slice(i, i + RT)
            x = dot_nt(kh[rs, :e], w_ref[0, j:e, :e]) + dot_nt(kh[rs, :e], w_ref[1, j:e, :e]) + dot_nt(kl[rs, :e], w_ref[0, j:e, :e])
            h, l = split(x)
            lh[rs, j:e] = h
            ll[rs, j:e] = l
    own = pl.ds(pl.multiple_of(q * B, B), B)
    fac_ref[...] = lh[:, own].astype(f32) + ll[:, own].astype(f32)
    @pl.when(p * B < lead)
    def _():
        ri = lax.broadcasted_iota(jnp.int32, (B, B), 0) + p * B
        ci = lax.broadcasted_iota(jnp.int32, (B, B), 1) + q * B
        fac_ref[:B, :] = jnp.where(ri >= ci, fac_ref[:B, :], 0.0)
    gsq = [None] * (lead // 256)
    for i in range(0, rows, RT):
        rs = slice(i, i + RT)
        tot = None
        for j in range(0, lead, 256):
            x = dot(lh[rs, j:], w_ref[0, j:, j:j+256]) + dot(lh[rs, j:], w_ref[1, j:, j:j+256]) + dot(ll[rs, j:], w_ref[0, j:, j:j+256])
            h, l = split(x)
            gh[rs, j:j+256] = h
            gl[rs, j:j+256] = l
            sm = jnp.sum(x, axis=1, keepdims=True)
            tot = sm if tot is None else tot + sm
            xx = x * x
            if i == 0:
                live = jnp.where(p * B < lead, 0.0, 1.0)
                xx = jnp.concatenate([xx[:B] * live, xx[B:]], axis=0)
            sq = jnp.sum(xx, axis=0, keepdims=True)
            n = j // 256
            gsq[n] = sq if gsq[n] is None else gsq[n] + sq
        g1[rs, :] = jnp.broadcast_to(tot, (RT, B))
    nzs = nz_ref[...]
    limit = jnp.sum(nzs * nzs) * (0.0018 ** 2 * rows * CT / float(nzs.shape[0] * B) ** 2)
    gs = jnp.broadcast_to(jnp.concatenate(gsq, axis=1), (8, lead))
    loads[3].wait()
    nch = 4 * half // CT
    bc = CT // B
    per = half // CT
    def col_block(c, u):
        g = c // per
        return 2 * ((g % 2) * (half // B) + (c % per) * bc + u) + g // 2
    def copies(c, slot, i):
        return [pltpu.make_async_copy(stage.at[slot, pl.ds(i, RT), pl.ds(u * B, B)],
                                      out_ref.at[pl.ds(i, RT), col_block(c, u), 0, :], sem.at[slot, i // RT, u]) for u in range(bc)]
    LT = 256
    def finish(c, slot, i):
        for u in range(bc):
            gb = col_block(c, u) * ncol + q
            a = gb // nrow
            @pl.when((gb % nrow == p) & (a * B >= i) & (a * B < i + RT))
            def _():
                r0 = pl.multiple_of(a * B, B)
                ri = lax.broadcasted_iota(jnp.int32, (B, B), 0)
                ci = lax.broadcasted_iota(jnp.int32, (B, B), 1)
                nzv = nz_ref[pl.ds(gb, 1), :]
                at = (slot, pl.ds(r0, B), slice(u*B, (u+1)*B))
                stage[at] = stage[at] + jnp.where(ri == ci, jnp.broadcast_to(nzv, (B, B)), 0.0)
            @pl.when(gb * B < lead)
            def _():
                stage[slot, i:i+RT, u*B:(u+1)*B] = jnp.zeros((RT, B), f32)
        if i == 0:
            @pl.when(p * B < lead)
            def _():
                stage[slot, :B, :] = jnp.zeros((B, CT), f32)
        for cp in copies(c, slot, i): cp.start()

    def chunk(c, _):
        slot = lax.rem(c, 2)
        c0 = pl.multiple_of((c % per) * CT, CT)
        zc = zc_ref[c // per, :, pl.ds(c0, CT)]
        x = zc.astype(f32)
        hc = jnp.sum(x * x, axis=0, keepdims=True) * cs
        mu = None
        gd = None
        for i in range(0, lead, LT):
            kc = jnp.exp2(dot(zlt[i:i+LT, :], zc) * (2 * cs) - wide(hlc[i:i+LT, :], CT) - hc)
            if mu is None:
                mu = jnp.mean(kc, axis=0, keepdims=True)
                mus[...] = jnp.broadcast_to(mu, (8, CT))
            dd = kc - mu
            dh[i:i+LT, :] = dd.astype(bf16)
            d2 = dd * dd
            ds = None
            for u in range(bc):
                live = jnp.where((col_block(c, u) * ncol + q) * B < lead, 0.0, 1.0)
                du = d2[:, u*B:(u+1)*B] * live
                ds = du if ds is None else ds + du
            part = dot(gs[:, i:i+LT], ds)
            gd = part if gd is None else gd + part
        err = jnp.sum(gd) * (1.0 / 8) * (2.0 * 2.0 ** -19)
        good = err <= limit
        @pl.when(c >= 2)
        def _():
            for i in range(0, rows, RT):
                for cp in copies(c, slot, i): cp.wait()
        @pl.when(good)
        def _():
            for i in range(0, rows, RT):
                rs = slice(i, i + RT)
                k = jnp.exp2(dot(zrt[rs, :], zc) * (2 * cs) - wide(hr[rs, :], CT) - hc)
                stage[slot, rs, :] = k - dot(gh[rs, :], dh[...]) - wide(g1[rs, :], CT) * mu
                finish(c, slot, i)
        @pl.when(jnp.logical_not(good))
        def _():
            def rowtile(n, _):
                rs = pl.ds(pl.multiple_of(n * 256, 256), 256)
                k = jnp.exp2(dot(zrt[rs, :], zc) * (2 * cs) - wide(hr[rs, :], CT) - hc)
                stage[slot, rs, :] = k - wide(g1[rs, :], CT) * mu
                return 0
            lax.fori_loop(0, rows // 256, rowtile, 0)
            def leadtile(m, _):
                ls = pl.ds(pl.multiple_of(m * LT, LT), LT)
                dd = jnp.exp2(dot(zlt[ls, :], zc) * (2 * cs) - wide(hlc[ls, :], CT) - hc) - mus[0:1, :]
                h, l = split(dd)
                def rt(n, _):
                    rs = pl.ds(pl.multiple_of(n * 256, 256), 256)
                    stage[slot, rs, :] = stage[slot, rs, :] - (dot(gh[rs, ls], h) + dot(gh[rs, ls], l) + dot(gl[rs, ls], h))
                    return 0
                lax.fori_loop(0, rows // 256, rt, 0)
                return 0
            lax.fori_loop(0, lead // LT, leadtile, 0)
            for i in range(0, rows, RT):
                finish(c, slot, i)
        return 0
    lax.fori_loop(0, nch, chunk, 0)
    for c in (nch - 2, nch - 1):
        for i in range(0, rows, RT):
            for cp in copies(c, c % 2, i): cp.wait()

def main_call(zl, zr, zc, w, nz, nrow=16, ncol=8):
    width, lead = zl.shape; half = zr.shape[2]; rows = 2 * half; cols = 4 * half
    V = pl.BlockSpec(memory_space=pltpu.VMEM)
    H = pl.BlockSpec(memory_space=pltpu.HBM)
    CT = 768
    return pl.pallas_call(functools.partial(main_body, width=width, lead=lead, nrow=nrow, ncol=ncol, CT=CT),
        out_shape=(jax.ShapeDtypeStruct((rows, cols // B, 1, B), f32), jax.ShapeDtypeStruct((rows, B), f32)),
        in_specs=[H, H, H, H, V],
        out_specs=(H, V),
        scratch_shapes=[pltpu.VMEM(zl.shape, bf16), pltpu.VMEM(zr.shape, bf16), pltpu.VMEM(zc.shape, bf16), pltpu.VMEM(w.shape, bf16),
          pltpu.VMEM((lead, width), bf16), pltpu.VMEM((rows, width), bf16)] +
          [pltpu.VMEM((rows, lead), bf16)] * 6 + [pltpu.VMEM((lead, CT), bf16), pltpu.VMEM((8, CT), f32)] +
          [pltpu.VMEM((rows, B), f32)] * 2 + [pltpu.VMEM((lead, B), f32),
          pltpu.VMEM((2, rows, CT), f32), pltpu.SemaphoreType.DMA((4,)), pltpu.SemaphoreType.DMA((2, 3, CT // B))],
        compiler_params=pltpu.CompilerParams(vmem_limit_bytes=61*2**20),
    )(zl, zr, zc, w, nz)


def body(embeddings, inv_scale, noise):
    nrow = lax.axis_size("row")
    ncol = lax.axis_size("col")
    total, fdev = embeddings.shape
    width = inv_scale.shape[0]
    crow = total // (TILE * nrow)
    ccol = total // (TILE * ncol)
    lead = PANELS * PB
    nz = noise.reshape(total // TILE, TILE)
    zl, zr, zc, w = lead_call(embeddings.T, inv_scale.reshape(width // TILE, TILE), nz, lead, width)
    half = zr.shape[-1]
    schur, factor = main_call(zl, zr.reshape(2, width, half), zc.reshape(4, width, half), w, nz,
                              nrow=nrow, ncol=ncol)
    return (
        factor.reshape(crow, 1, TILE, TILE),
        schur.reshape(crow, 1, TILE, ccol, 1, TILE),
    )


def solution(mesh):
    placed = (P(None, ("row", "col")), P(), P())
    return jax.shard_map(
        body,
        mesh=mesh,
        in_specs=placed,
        out_specs=(P(None, "row", None, "col"), P(None, "row", None, None, "col", None)),
        check_vma=False,
    )
```
